128 devices in a mesh: row: 8 (over y, z_lo), col: 16 (over x, z_hi, core).
Axes of the slice: x: 4, y: 4, z: 4 (z_hi: 2, z_lo: 2; z = z_hi * 2 + z_lo), core: 2. Of those that a mesh axis runs over, the one named last changes fastest.
Arguments:
- pair_rep: bfloat16 [512, 512, 128], P('row', 'col'), may hold values from -6 to 6
- side_weight: bfloat16 [2, 2, 2, 128, 128], replicated, may hold values from -0.5 to 0.5
- gate_weight: bfloat16 [2, 128, 128], replicated, may hold values from -0.5 to 0.5
- out_weight: bfloat16 [2, 128, 128], replicated, may hold values from -0.5 to 0.5
- in_gain: float32 [2, 128], replicated, may hold values from 0.1 to 1.9
- out_gain: float32 [2, 128], replicated, may hold values from 0.1 to 1.9
Outputs:
- updated_pair: bfloat16 [512, 512, 128], P('row', 'col')
The draws below stay inside these ranges and needn't reach their ends.
All inputs are finite; a program needn't handle non-finite values.
Results may differ from the reference program's by a relative error of at most 0.018.
Values may be sent and summed in bfloat16 or wider, within the bound.
No kernel may reach another device: no remote copies, remote signals or barrier semaphores. Data moves between devices by JAX's collectives and lax.ppermute only.
A program may use at most 64 MiB of HBM per device.

```python
import math
import jax
import jax.numpy as jnp
from jax import lax

C = 128
HID = 128
N = 512


def block_levels(key, dims, pieces, smallest, high):
    gain, own = 1.0, jax.random.fold_in(key, 6)
    for position, parts in pieces:
        heights = jnp.exp(jax.random.uniform(jax.random.fold_in(own, position), (parts,), jnp.float32, smallest / len(pieces), high / len(pieces)))
        gain = gain * jnp.repeat(heights, dims[position] // parts).reshape([-1 if axis == position else 1 for axis in range(len(dims))])
    return gain


def gaussian(own_key, dims, spread, reach, pieces=(), kind=jnp.bfloat16):
    entries = jax.random.normal(own_key, dims, jnp.float32) * spread
    if len(pieces) > 0:
        entries = block_levels(own_key, dims, pieces, -0.22, 0.18) * entries
    return jnp.clip(entries, min=-reach, max=reach).astype(kind)


def setup_inputs(seed: int = 0) -> dict:
    arg_keys = jax.random.split(jax.random.key(seed), 7)
    pair_rep = gaussian(arg_keys[0], (N, N, C), 1.0, 6.0, ((0, 8), (1, 16)))
    side_weight = gaussian(arg_keys[1], (2, 2, 2, C, HID), C ** -0.5, 0.5)
    gate_weight = gaussian(arg_keys[2], (2, C, C), C ** -0.5, 0.5)
    out_weight = gaussian(arg_keys[3], (2, HID, C), HID ** -0.5, 0.5)
    in_gain = jnp.clip(1.0 + 0.18 * jax.random.normal(arg_keys[4], (2, C), jnp.float32), 0.1, 1.9)
    out_gain = jnp.clip(1.0 + 0.18 * jax.random.normal(arg_keys[5], (2, HID), jnp.float32), 0.1, 1.9)
    return dict(pair_rep=pair_rep, side_weight=side_weight, gate_weight=gate_weight, out_weight=out_weight, in_gain=in_gain, out_gain=out_gain)


epsilon = 1e-05

def layer_norm(values, gain_row, axis_pos):
    average = lax.optimization_barrier(jnp.mean(values, axis=axis_pos, keepdims=True))
    centred = values - average
    variance = lax.optimization_barrier(jnp.mean(centred * centred, axis=axis_pos, keepdims=True))
    return centred * lax.rsqrt(variance + epsilon) * gain_row

def reference(pair_rep, side_weight, gate_weight, out_weight, in_gain, out_gain):
    block_rows = math.gcd(N, 128)
    block_count = N // block_rows
    current = pair_rep
    for update in range(2):
        blocks = current.reshape(block_count, block_rows, N, C)

        def project(rows_in):
            normed = layer_norm(rows_in.astype(jnp.float32), in_gain[update], -1).astype(jnp.bfloat16)
            flat_rows = normed.reshape(block_rows * N, C)
            side_list = []
            for side_idx in range(2):
                value_part = jnp.dot(flat_rows, side_weight[update, side_idx, 0], preferred_element_type=jnp.float32)
                gate_part = jnp.dot(flat_rows, side_weight[update, side_idx, 1], preferred_element_type=jnp.float32)
                side_val = (jax.nn.sigmoid(gate_part) * value_part).astype(jnp.bfloat16)
                side_list.append(side_val.reshape(block_rows, N, HID))
            return (side_list[0], side_list[1])
        left_rows, right_rows = lax.map(project, blocks)
        left_all = jnp.transpose(left_rows.reshape(N, N, HID), (2, 0, 1))
        right_all = jnp.transpose(right_rows.reshape(N, N, HID), (2, 0, 1))

        def triangle(operands):
            left_chan, right_chan = operands
            if update == 0:
                product_mat = jnp.dot(left_chan, right_chan.T, preferred_element_type=jnp.float32)
            else:
                product_mat = jnp.dot(left_chan.T, right_chan, preferred_element_type=jnp.float32)
            return product_mat.astype(jnp.bfloat16)
        mixed_all = lax.map(triangle, (left_all, right_all))
        mixed_rows = jnp.transpose(mixed_all, (1, 2, 0)).reshape(block_count, block_rows, N, HID)

        def finish(operands):
            rows_in, mixed_block = operands
            normed = layer_norm(rows_in.astype(jnp.float32), in_gain[update], -1).astype(jnp.bfloat16)
            gate_vals = jax.nn.sigmoid(jnp.dot(normed.reshape(-1, C), gate_weight[update], preferred_element_type=jnp.float32))
            out_normed = layer_norm(mixed_block.astype(jnp.float32), out_gain[update], -1).astype(jnp.bfloat16)
            change = jnp.dot(out_normed.reshape(-1, HID), out_weight[update], preferred_element_type=jnp.float32)
            summed = rows_in.astype(jnp.float32).reshape(-1, C) + gate_vals * change
            return summed.astype(jnp.bfloat16).reshape(block_rows, N, C)
        current = lax.map(finish, (blocks, mixed_rows)).reshape(N, N, C)
    return current
```

```python
import functools

import jax
import jax.numpy as jnp
import numpy as np
from jax import lax
from jax.experimental import pallas as pl
from jax.experimental.pallas import tpu as pltpu
from jax.sharding import PartitionSpec as P

epsilon = 1e-05
F32 = jnp.float32
BF16 = jnp.bfloat16

BITS = ("y_hi", "y_lo", "z_lo", "x_hi", "x_lo", "z_hi", "core")
ORDER = BITS


def device_number(r, c):
    return 16 * r + c


def dot(a, b, dims):
    return lax.dot_general(a, b, (dims, ((), ())), preferred_element_type=F32)


def ahead(items, produce, consume):
    waiting = None
    for item in items:
        made = produce(item)
        if waiting is not None:
            consume(*waiting)
        waiting = (item, made)
    consume(*waiting)


def two_blocks(matrix):
    zero = jnp.zeros_like(matrix)
    return jnp.concatenate(
        [jnp.concatenate([matrix, zero], axis=1), jnp.concatenate([zero, matrix], axis=1)], axis=0
    )


def side_by_side(ref, n):
    return jnp.concatenate([ref[n : n + 512, :], ref[n + 512 : n + 1024, :]], axis=1)


def norm_rows(pair_ref, gain, centred_ref, normed_ref):
    row = lax.broadcasted_iota(jnp.int32, (128, 128), 0)
    column = lax.broadcasted_iota(jnp.int32, (128, 128), 1)
    centring = two_blocks(jnp.where(row == column, 127.0 / 128.0, -1.0 / 128.0).astype(BF16))
    average = two_blocks(jnp.full((128, 128), 1.0 / 128.0, BF16))
    gains = jnp.concatenate([gain, gain], axis=1)
    for n in range(0, 2048, 1024):
        centred_ref[n // 2 : n // 2 + 512, :] = dot(side_by_side(pair_ref, n), centring, ((1,), (0,)))

    def spread(n):
        centred = centred_ref[n // 2 : n // 2 + 512, :]
        return dot((centred * centred).astype(BF16), average, ((1,), (0,)))

    def scale(n, variance):
        normed = (centred_ref[n // 2 : n // 2 + 512, :] * lax.rsqrt(variance + epsilon) * gains).astype(BF16)
        normed_ref[n : n + 512, :] = normed[:, :128]
        normed_ref[n + 512 : n + 1024, :] = normed[:, 128:]

    ahead(range(0, 2048, 1024), spread, scale)


def swap_matrix():
    row = lax.broadcasted_iota(jnp.int32, (256, 256), 0)
    column = lax.broadcasted_iota(jnp.int32, (256, 256), 1)
    return jnp.where((row & 15) * 16 + (row >> 4) == column, 1.0, 0.0).astype(BF16)


def emit_sides(half_ref, swap, out_ref):
    def swapped(channel):
        return dot(swap, half_ref[:, channel : channel + 16, :].reshape(256, 256), ((1,), (0,))).astype(BF16)

    def store(channel, both):
        for side in range(2):
            part = both[:, 128 * side : 128 * side + 128].reshape(16, 16, 128)
            out_ref[channel : channel + 16, side] = part

    ahead(range(0, 128, 16), swapped, store)


def project(pair_ref, gain, wt_ref, gate_weight, swap, refs, out_ref, gate_ref, strided=False):
    centred_ref, normed_ref, half_ref = refs
    norm_rows(pair_ref, gain, centred_ref, normed_ref)
    slabs = normed_ref.reshape(4, 16, 32, 128)
    def product(place):
        s, side = place
        normed = jnp.concatenate([slabs[:, s + n].reshape(128, 128) for n in range(2)], axis=0)
        return dot(wt_ref[256 * side : 256 * side + 256], normed, ((1,), (1,))).reshape(16, 2, 8, 256)

    def gated(place, both):
        s, side = place
        result = (both[:, 0] + both[:, 0] * jnp.tanh(both[:, 1])).reshape(128, 256)
        for n in range(2):
            if strided:
                half_ref[pl.ds(side * 16 + s + n, 128, stride=40), :] = result[:, 128 * n : 128 * n + 128]
                continue
            result = result.astype(BF16)
            half_ref[s + n, :, 128 * side : 128 * side + 128] = result[:, 128 * n : 128 * n + 128]

    ahead([(s, side) for s in range(0, 16, 2) for side in range(2)], product, gated)
    weight = two_blocks(halved(gate_weight))

    def gate_product(n):
        return dot(side_by_side(normed_ref, n), weight, ((1,), (0,)))

    def gate(n, values):
        values = jnp.tanh(values)
        gate_ref[n : n + 512, :] = values[:, :128]
        gate_ref[n + 512 : n + 1024, :] = values[:, 128:]

    ahead(range(0, 2048, 1024), gate_product, gate)
    if strided:
        for channel in range(0, 128, 16):
            part = half_ref[channel * 40 : channel * 40 + 640, :].reshape(16, 40, 128)[:, :32]
            out_ref[channel : channel + 16] = part.astype(BF16).reshape(16, 2, 16, 128)
    else:
        emit_sides(half_ref, swap, out_ref)


def halved(weight):
    return (0.5 * weight.astype(F32)).astype(BF16)


def fill_weights(side_ref, wt_ref, update):
    for side in range(2):
        value, gate = [
            (0.5 * side_ref[4 * update + 2 * side + n].astype(F32)).T.reshape(16, 1, 8, 128) for n in range(2)
        ]
        both = jnp.concatenate([value, gate], axis=1).reshape(256, 128)
        wt_ref[256 * side : 256 * side + 256, :] = both.astype(BF16)


def project_kernel(
    pair_hbm, side_hbm, gate_weight_hbm, gain_hbm, out_gain_hbm, out_ref, gate_ref, gain_ref, pair_ref, side_ref, gate_weight_ref,
    wt_ref, centred_ref, normed_ref, half_ref, sems,
):
    copies = [
        pltpu.make_async_copy(side_hbm.at[pl.ds(0, 4)], side_ref, sems.at[0]),
        pltpu.make_async_copy(pair_hbm, pair_ref, sems.at[1]),
        pltpu.make_async_copy(gate_weight_hbm.at[0], gate_weight_ref, sems.at[2]),
        pltpu.make_async_copy(gain_hbm, gain_ref.at[0], sems.at[3]),
        pltpu.make_async_copy(out_gain_hbm, gain_ref.at[1], sems.at[4]),
    ]
    for copy in copies:
        copy.start()
    copies[0].wait()
    fill_weights(side_ref, wt_ref, 0)
    for copy in copies[1:]:
        copy.wait()
    project(
        pair_ref, gain_ref[0, 0:1, :], wt_ref, gate_weight_ref[...], None,
        (centred_ref, normed_ref, half_ref), out_ref, gate_ref, True,
    )


def swap_groups(groups, low, even):
    halves = [pair for t in groups for pair in ((t[0], t[2]), (t[1], t[3]))]
    moved = [pltpu.roll(jnp.where(low, b, a), 64, 1) for a, b in halves]
    halves = [(jnp.where(low, a, m), jnp.where(low, m, b)) for (a, b), m in zip(halves, moved)]
    crossed = []
    for (u0, u2), (u1, u3) in zip(halves[::2], halves[1::2]):
        crossed += [(u0, u1), (u2, u3)]
    rolled = [(pltpu.roll(b, 32, 1), pltpu.roll(a, 96, 1)) for a, b in crossed]
    out = [
        (jnp.where(even, a, to_first), jnp.where(even, to_second, b))
        for (a, b), (to_first, to_second) in zip(crossed, rolled)
    ]
    return [first + second for first, second in zip(out[::2], out[1::2])]


def triangle_kernel(in_ref, regroup_ref, out_ref, left_ref, right_ref, *, update):
    lane = lax.broadcasted_iota(jnp.int32, (16, 128), 1)
    low = lane < 64
    even = (lane & 32) == 0


    def stacked(side, places):
        tiles = []
        for n in range(4):
            numbers = [device_number(r, 4 * block + n) for r, block in places]
            tiles.append(jnp.concatenate([in_ref[32 * m + 16 * side : 32 * m + 16 * side + 16, :] for m in numbers], axis=0))
        return jnp.concatenate(tiles, axis=1)

    for half in range(2):
        if update == 0:
            places = [(4 * half + r, block) for r in range(4) for block in range(4)]
            regrouped = dot(stacked(1, places), regroup_ref[...], ((1,), (0,))).astype(BF16)
            for m, (r, block) in enumerate(places):
                for g in range(4):
                    row = r * 64 + g * 16
                    tile = regrouped[16 * m : 16 * m + 16, 128 * g : 128 * g + 128]
                    right_ref[row : row + 16, 128 * block : 128 * block + 128] = tile
        else:
            places = [(r, 2 * half + block) for block in range(2) for r in range(8)]
            regrouped = dot(regroup_ref[...], stacked(0, places), ((1,), (1,))).astype(BF16)
            for block in range(2):
                for g in range(4):
                    row = 128 * (2 * half + block)
                    tile = regrouped[128 * g : 128 * g + 128, 128 * block : 128 * block + 128]
                    left_ref[row : row + 128, 128 * g : 128 * g + 128] = tile
    side, full_ref = ((0, left_ref), (1, right_ref))[update]
    places = [(r, block) for r in range(8) for block in range(4)]
    groups = []
    for r, block in places:
        numbers = [device_number(r, 4 * block + n) for n in range(4)]
        groups.append([in_ref[32 * m + 16 * side : 32 * m + 16 * side + 16, :] for m in numbers])
    for (r, block), tiles in zip(places, swap_groups(groups, low, even)):
        for g, tile in enumerate(tiles):
            row = r * 64 + g * 16 if update == 0 else g * 128 + r * 16
            full_ref[row : row + 16, 128 * block : 128 * block + 128] = tile
    products = []
    for half in range(2):
        part = slice(256 * half, 256 * half + 256)
        if update == 0:
            products.append(dot(left_ref[...], right_ref[part, :], ((1,), (1,))).astype(BF16))
        else:
            products.append(dot(left_ref[...], right_ref[:, part], ((1,), (0,))).astype(BF16))
    for half, mixed in enumerate(products):
        places = [(r, block) for r in range(8) for block in range(2)]
        groups = [
            [mixed[r * 64 + 16 * g : r * 64 + 16 * g + 16, 128 * block : 128 * block + 128] for g in range(4)]
            for r, block in places
        ]
        for (r, block), tiles in zip(places, swap_groups(groups, low, even)):
            for n, tile in enumerate(tiles):
                row = device_number(r, 8 * half + 4 * block + n) * 16
                out_ref[row : row + 16, :] = tile


def finish_kernel(mixed_ref, pair_ref, gate_ref, out_weight_ref, gain_ref, *rest, update):
    if update == 0:
        (side_ref, gate_weight_ref, pair_out_ref, out_ref, gate_out_ref, raw_ref, wt_ref, centred_ref,
         normed_ref, half_ref) = rest
    else:
        pair_hbm, raw_ref, pair_out_ref, sems = rest
    if update == 0:
        fill_weights(side_ref, wt_ref, 1)
    swap = swap_matrix()

    def swapped(row):
        pieces = [mixed_ref[row + 256 * n : row + 256 * n + 256, :] for n in range(2)]
        return dot(swap, jnp.concatenate(pieces, axis=1), ((1,), (0,)))

    def store(row, both):
        for n in range(2):
            channel = row // 16 + 16 * n
            raw_ref[:, channel : channel + 16, :] = both[:, 128 * n : 128 * n + 128].reshape(16, 16, 128)

    ahead(range(0, 2048, 512), swapped, store)
    out_gain = jnp.broadcast_to(gain_ref[1, update : update + 1, :], (128, 128)).T
    weight = two_blocks(halved(out_weight_ref[update]))
    slabs = [ref.reshape(4, 16, 32, 128) for ref in (pair_ref, gate_ref, pair_out_ref)]
    copies = []
    out_normed = {}
    for s in range(0, 18, 2):
        if s < 16:
            values = raw_ref[s : s + 2]
            centred = values - jnp.mean(values, axis=1, keepdims=True)
            variance = jnp.mean(centred * centred, axis=1, keepdims=True)
            out_normed[s] = (centred * lax.rsqrt(variance + epsilon) * out_gain).astype(BF16)
        if s == 0:
            continue
        changes = dot(out_normed[s - 2].reshape(256, 128), weight, ((0,), (0,)))
        for n in range(2):
            change = changes[:, 128 * n : 128 * n + 128].reshape(4, 32, 128)
            before, gate = slabs[0][:, s - 2 + n].astype(F32), slabs[1][:, s - 2 + n]
            slabs[2][:, s - 2 + n] = (before + (change + change * gate)).astype(BF16)
        if update == 1 and s % 4 == 0:
            part = pl.ds(s - 4, 4)
            copies.append(pltpu.make_async_copy(slabs[2].at[:, part], pair_hbm.at[:, part], sems.at[s // 4 - 1]))
            copies[-1].start()
    for copy in copies:
        copy.wait()
    if update == 0:
        project(
            pair_out_ref, gain_ref[0, 1:2, :], wt_ref, gate_weight_ref[1], swap,
            (centred_ref, normed_ref, half_ref), out_ref, gate_out_ref,
        )


def call(kernel, out, scratch, *operands, hbm=(), hbm_out=False):
    operands = [pltpu.with_memory_space_constraint(a, pltpu.HBM) if n in hbm else a for n, a in enumerate(operands)]
    spaces = [pltpu.HBM if n in hbm else pltpu.VMEM for n in range(len(operands))]
    return pl.pallas_call(
        kernel,
        out_shape=[jax.ShapeDtypeStruct(*one) for one in out],
        in_specs=[pl.BlockSpec(memory_space=space) for space in spaces],
        out_specs=[pl.BlockSpec(memory_space=pltpu.HBM if hbm_out else pltpu.VMEM) for _ in out],
        scratch_shapes=[pltpu.VMEM(*one) if isinstance(one, tuple) else one for one in scratch],
        compiler_params=pltpu.CompilerParams(vmem_limit_bytes=32 * 1024 * 1024),
    )(*operands)


SIDES = ((128, 2, 16, 128), BF16)
MIXED = ((2048, 128), BF16)
PAIR = ((2048, 128), BF16)
GATE = ((2048, 128), F32)
GAIN = ((2, 2, 128), F32)
PROJECT_SCRATCH = [((512, 128), BF16), ((1024, 256), F32), ((2048, 128), BF16), ((16, 128, 256), BF16)]


def exchange(flat):
    pieces = flat.reshape(128, -1, 128)
    moved = lax.all_to_all(pieces, ORDER, split_axis=0, concat_axis=0, tiled=True)
    return moved.reshape(-1, 128)


def on_device(pair_rep, side_weight, gate_weight, out_weight, in_gain, out_gain):
    pair = pair_rep.reshape(PAIR[0])
    side_weight = side_weight.reshape(8, 128, 128)
    sides, gate, gains = call(
        project_kernel,
        [SIDES, GATE, GAIN],
        [PAIR, ((4, 128, 128), BF16), ((128, 128), BF16), *PROJECT_SCRATCH[:-1], ((5120, 128), F32), pltpu.SemaphoreType.DMA((5,))],
        pair, side_weight, gate_weight, in_gain, out_gain,
        hbm=range(5),
    )
    regroup = jnp.asarray(np.eye(512).reshape(4, 4, 32, 512).transpose(1, 0, 2, 3).reshape(512, 512).T, BF16)
    finish_scratch = [((16, 128, 128), F32)]
    for update in range(2):
        sides = exchange(sides)
        triangle = functools.partial(triangle_kernel, update=update)
        (mixed,) = call(triangle, [MIXED], [((512, 512), BF16)] * 2, sides, regroup)
        mixed = exchange(mixed)
        finish = functools.partial(finish_kernel, update=update)
        operands = (mixed, pair, gate, out_weight, gains)
        if update == 0:
            pair, sides, gate = call(
                finish, [PAIR, SIDES, GATE], finish_scratch + PROJECT_SCRATCH,
                *operands, side_weight, gate_weight,
            )
        else:
            scratch = finish_scratch + [PAIR, pltpu.SemaphoreType.DMA((4,))]
            (pair,) = call(finish, [((4, 16, 32, 128), BF16)], scratch, *operands, hbm_out=True)
    return pair.reshape(pair_rep.shape)


def solution(mesh):
    physical = jax.sharding.Mesh(mesh.devices.reshape((2,) * 7), BITS)
    tile = P(BITS[:3], BITS[3:], None)
    return jax.shard_map(
        on_device, mesh=physical, in_specs=(tile, P(), P(), P(), P(), P()), out_specs=tile, check_vma=False
    )
```

```python
import functools

import jax
import jax.numpy as jnp
import numpy as np
from jax import lax
from jax.experimental import pallas as pl
from jax.experimental.pallas import tpu as pltpu
from jax.sharding import PartitionSpec as P

epsilon = 1e-05
F32 = jnp.float32
BF16 = jnp.bfloat16

BITS = ("y_hi", "y_lo", "z_lo", "x_hi", "x_lo", "z_hi", "core")
ORDER = BITS


def device_number(r, c):
    return 16 * r + c


def dot(a, b, dims):
    return lax.dot_general(a, b, (dims, ((), ())), preferred_element_type=F32)


def ahead(items, produce, consume):
    waiting = None
    for item in items:
        made = produce(item)
        if waiting is not None:
            consume(*waiting)
        waiting = (item, made)
    consume(*waiting)


def two_blocks(matrix):
    zero = jnp.zeros_like(matrix)
    return jnp.concatenate(
        [jnp.concatenate([matrix, zero], axis=1), jnp.concatenate([zero, matrix], axis=1)], axis=0
    )


def side_by_side(ref, n):
    return jnp.concatenate([ref[n : n + 512, :], ref[n + 512 : n + 1024, :]], axis=1)


def norm_rows(pair_ref, gain, centred_ref, normed_ref):
    row = lax.broadcasted_iota(jnp.int32, (128, 128), 0)
    column = lax.broadcasted_iota(jnp.int32, (128, 128), 1)
    centring = two_blocks(jnp.where(row == column, 127.0 / 128.0, -1.0 / 128.0).astype(BF16))
    average = two_blocks(jnp.full((128, 128), 1.0 / 128.0, BF16))
    gains = jnp.concatenate([gain, gain], axis=1)
    for n in range(0, 2048, 1024):
        centred_ref[n // 2 : n // 2 + 512, :] = dot(side_by_side(pair_ref, n), centring, ((1,), (0,)))

    def spread(n):
        centred = centred_ref[n // 2 : n // 2 + 512, :]
        return dot((centred * centred).astype(BF16), average, ((1,), (0,)))

    def scale(n, variance):
        normed = (centred_ref[n // 2 : n // 2 + 512, :] * lax.rsqrt(variance + epsilon) * gains).astype(BF16)
        normed_ref[n : n + 512, :] = normed[:, :128]
        normed_ref[n + 512 : n + 1024, :] = normed[:, 128:]

    ahead(range(0, 2048, 1024), spread, scale)


def swap_matrix():
    row = lax.broadcasted_iota(jnp.int32, (256, 256), 0)
    column = lax.broadcasted_iota(jnp.int32, (256, 256), 1)
    return jnp.where((row & 15) * 16 + (row >> 4) == column, 1.0, 0.0).astype(BF16)


def project(pair_ref, gain, wt_ref, gate_weight, refs, out_ref, gate_ref):
    centred_ref, normed_ref, half_ref = refs
    norm_rows(pair_ref, gain, centred_ref, normed_ref)
    slabs = normed_ref.reshape(4, 16, 32, 128)
    def product(place):
        s, side = place
        normed = jnp.concatenate([slabs[:, s + n].reshape(128, 128) for n in range(2)], axis=0)
        return dot(wt_ref[256 * side : 256 * side + 256], normed, ((1,), (1,))).reshape(16, 2, 8, 256)

    def gated(place, both):
        s, side = place
        result = (both[:, 0] + both[:, 0] * jnp.tanh(both[:, 1])).reshape(128, 256)
        for n in range(2):
            half_ref[pl.ds(side * 16 + s + n, 128, stride=40), :] = result[:, 128 * n : 128 * n + 128]

    ahead([(s, side) for s in range(0, 16, 2) for side in range(2)], product, gated)
    weight = two_blocks(halved(gate_weight))

    def gate_product(n):
        return dot(side_by_side(normed_ref, n), weight, ((1,), (0,)))

    def gate(n, values):
        values = jnp.tanh(values)
        gate_ref[n : n + 512, :] = values[:, :128]
        gate_ref[n + 512 : n + 1024, :] = values[:, 128:]

    ahead(range(0, 2048, 1024), gate_product, gate)
    for channel in range(0, 128, 16):
        part = half_ref[channel * 40 : channel * 40 + 640, :].reshape(16, 40, 128)[:, :32]
        out_ref[channel : channel + 16] = part.astype(BF16).reshape(16, 2, 16, 128)


def halved(weight):
    return (0.5 * weight.astype(F32)).astype(BF16)


def fill_weights(side_ref, wt_ref, update):
    for side in range(2):
        value, gate = [
            (0.5 * side_ref[4 * update + 2 * side + n].astype(F32)).T.reshape(16, 1, 8, 128) for n in range(2)
        ]
        both = jnp.concatenate([value, gate], axis=1).reshape(256, 128)
        wt_ref[256 * side : 256 * side + 256, :] = both.astype(BF16)


def project_kernel(
    pair_hbm, side_hbm, gate_weight_hbm, gain_hbm, out_gain_hbm, out_ref, gate_ref, gain_ref, pair_ref, side_ref, gate_weight_ref,
    wt_ref, centred_ref, normed_ref, half_ref, sems,
):
    copies = [
        pltpu.make_async_copy(side_hbm.at[pl.ds(0, 4)], side_ref, sems.at[0]),
        pltpu.make_async_copy(pair_hbm, pair_ref, sems.at[1]),
        pltpu.make_async_copy(gate_weight_hbm.at[0], gate_weight_ref, sems.at[2]),
        pltpu.make_async_copy(gain_hbm, gain_ref.at[0], sems.at[3]),
        pltpu.make_async_copy(out_gain_hbm, gain_ref.at[1], sems.at[4]),
    ]
    for copy in copies:
        copy.start()
    copies[0].wait()
    fill_weights(side_ref, wt_ref, 0)
    for copy in copies[1:]:
        copy.wait()
    project(
        pair_ref, gain_ref[0, 0:1, :], wt_ref, gate_weight_ref[...],
        (centred_ref, normed_ref, half_ref), out_ref, gate_ref,
    )


def swap_groups(groups, low, even):
    halves = [pair for t in groups for pair in ((t[0], t[2]), (t[1], t[3]))]
    moved = [pltpu.roll(jnp.where(low, b, a), 64, 1) for a, b in halves]
    halves = [(jnp.where(low, a, m), jnp.where(low, m, b)) for (a, b), m in zip(halves, moved)]
    crossed = []
    for (u0, u2), (u1, u3) in zip(halves[::2], halves[1::2]):
        crossed += [(u0, u1), (u2, u3)]
    rolled = [(pltpu.roll(b, 32, 1), pltpu.roll(a, 96, 1)) for a, b in crossed]
    out = [
        (jnp.where(even, a, to_first), jnp.where(even, to_second, b))
        for (a, b), (to_first, to_second) in zip(crossed, rolled)
    ]
    return [first + second for first, second in zip(out[::2], out[1::2])]


def triangle_kernel(in_ref, regroup_ref, out_ref, left_ref, right_ref, *, update):
    lane = lax.broadcasted_iota(jnp.int32, (16, 128), 1)
    low = lane < 64
    even = (lane & 32) == 0


    def stacked(side, places):
        tiles = []
        for n in range(4):
            numbers = [device_number(r, 4 * block + n) for r, block in places]
            tiles.append(jnp.concatenate([in_ref[32 * m + 16 * side : 32 * m + 16 * side + 16, :] for m in numbers], axis=0))
        return jnp.concatenate(tiles, axis=1)

    for half in range(2):
        if update == 0:
            places = [(4 * half + r, block) for r in range(4) for block in range(4)]
            regrouped = dot(stacked(1, places), regroup_ref[...], ((1,), (0,))).astype(BF16)
            for m, (r, block) in enumerate(places):
                for g in range(4):
                    row = r * 64 + g * 16
                    tile = regrouped[16 * m : 16 * m + 16, 128 * g : 128 * g + 128]
                    right_ref[row : row + 16, 128 * block : 128 * block + 128] = tile
        else:
            places = [(r, 2 * half + block) for block in range(2) for r in range(8)]
            regrouped = dot(regroup_ref[...], stacked(0, places), ((1,), (1,))).astype(BF16)
            for block in range(2):
                for g in range(4):
                    row = 128 * (2 * half + block)
                    tile = regrouped[128 * g : 128 * g + 128, 128 * block : 128 * block + 128]
                    left_ref[row : row + 128, 128 * g : 128 * g + 128] = tile
    side, full_ref = ((0, left_ref), (1, right_ref))[update]
    places = [(r, block) for r in range(8) for block in range(4)]
    groups = []
    for r, block in places:
        numbers = [device_number(r, 4 * block + n) for n in range(4)]
        groups.append([in_ref[32 * m + 16 * side : 32 * m + 16 * side + 16, :] for m in numbers])
    for (r, block), tiles in zip(places, swap_groups(groups, low, even)):
        for g, tile in enumerate(tiles):
            row = r * 64 + g * 16 if update == 0 else g * 128 + r * 16
            full_ref[row : row + 16, 128 * block : 128 * block + 128] = tile
    products = []
    for half in range(2):
        part = slice(256 * half, 256 * half + 256)
        if update == 0:
            products.append(dot(left_ref[...], right_ref[part, :], ((1,), (1,))).astype(BF16))
        else:
            products.append(dot(left_ref[...], right_ref[:, part], ((1,), (0,))).astype(BF16))
    for half, mixed in enumerate(products):
        places = [(r, block) for r in range(8) for block in range(2)]
        groups = [
            [mixed[r * 64 + 16 * g : r * 64 + 16 * g + 16, 128 * block : 128 * block + 128] for g in range(4)]
            for r, block in places
        ]
        for (r, block), tiles in zip(places, swap_groups(groups, low, even)):
            for n, tile in enumerate(tiles):
                row = device_number(r, 8 * half + 4 * block + n) * 16
                out_ref[row : row + 16, :] = tile


def finish_kernel(mixed_ref, pair_ref, gate_ref, out_weight_ref, gain_ref, *rest, update):
    if update == 0:
        (side_ref, gate_weight_ref, pair_out_ref, out_ref, gate_out_ref, raw_ref, wt_ref, centred_ref,
         normed_ref, half_ref) = rest
    else:
        pair_hbm, raw_ref, pair_out_ref, sems = rest
    if update == 0:
        fill_weights(side_ref, wt_ref, 1)
    if update == 0:
        swap = swap_matrix()

        def swapped(row):
            pieces = [mixed_ref[row + 256 * n : row + 256 * n + 256, :] for n in range(2)]
            return dot(swap, jnp.concatenate(pieces, axis=1), ((1,), (0,)))

        def store(row, both):
            for n in range(2):
                channel = row // 16 + 16 * n
                raw_ref[:, channel : channel + 16, :] = both[:, 128 * n : 128 * n + 128].reshape(16, 16, 128)

        ahead(range(0, 2048, 512), swapped, store)
    else:
        for channel in range(0, 128, 16):
            part = mixed_ref[16 * channel : 16 * channel + 256, :].astype(F32).reshape(16, 16, 128)
            for n in range(16):
                raw_ref[24 * (channel + n) : 24 * (channel + n) + 16, :] = part[n]
    out_gain = jnp.broadcast_to(gain_ref[1, update : update + 1, :], (128, 128)).T
    weight = two_blocks(halved(out_weight_ref[update]))
    slabs = [ref.reshape(4, 16, 32, 128) for ref in (pair_ref, gate_ref, pair_out_ref)]
    copies = []
    out_normed = {}
    for s in range(0, 18, 2):
        if s < 16:
            if update == 0:
                values = raw_ref[s : s + 2]
            else:
                values = jnp.stack([raw_ref[pl.ds(s + n, 128, stride=24), :] for n in range(2)])
            centred = values - jnp.mean(values, axis=1, keepdims=True)
            variance = jnp.mean(centred * centred, axis=1, keepdims=True)
            out_normed[s] = (centred * lax.rsqrt(variance + epsilon) * out_gain).astype(BF16)
        if s == 0:
            continue
        changes = dot(out_normed[s - 2].reshape(256, 128), weight, ((0,), (0,)))
        for n in range(2):
            change = changes[:, 128 * n : 128 * n + 128].reshape(4, 32, 128)
            before, gate = slabs[0][:, s - 2 + n].astype(F32), slabs[1][:, s - 2 + n]
            slabs[2][:, s - 2 + n] = (before + (change + change * gate)).astype(BF16)
        if update == 1 and s % 4 == 0:
            part = pl.ds(s - 4, 4)
            copies.append(pltpu.make_async_copy(slabs[2].at[:, part], pair_hbm.at[:, part], sems.at[s // 4 - 1]))
            copies[-1].start()
    for copy in copies:
        copy.wait()
    if update == 0:
        project(
            pair_out_ref, gain_ref[0, 1:2, :], wt_ref, gate_weight_ref[1],
            (centred_ref, normed_ref, half_ref), out_ref, gate_out_ref,
        )


def call(kernel, out, scratch, *operands, hbm=(), hbm_out=False):
    operands = [pltpu.with_memory_space_constraint(a, pltpu.HBM) if n in hbm else a for n, a in enumerate(operands)]
    spaces = [pltpu.HBM if n in hbm else pltpu.VMEM for n in range(len(operands))]
    return pl.pallas_call(
        kernel,
        out_shape=[jax.ShapeDtypeStruct(*one) for one in out],
        in_specs=[pl.BlockSpec(memory_space=space) for space in spaces],
        out_specs=[pl.BlockSpec(memory_space=pltpu.HBM if hbm_out else pltpu.VMEM) for _ in out],
        scratch_shapes=[pltpu.VMEM(*one) if isinstance(one, tuple) else one for one in scratch],
        compiler_params=pltpu.CompilerParams(vmem_limit_bytes=32 * 1024 * 1024),
    )(*operands)


SIDES = ((128, 2, 16, 128), BF16)
MIXED = ((2048, 128), BF16)
PAIR = ((2048, 128), BF16)
GATE = ((2048, 128), F32)
GAIN = ((2, 2, 128), F32)
PROJECT_SCRATCH = [((512, 128), BF16), ((1024, 256), F32), ((2048, 128), BF16), ((5120, 128), F32)]


def exchange(flat):
    pieces = flat.reshape(128, -1, 128)
    moved = lax.all_to_all(pieces, ORDER, split_axis=0, concat_axis=0, tiled=True)
    return moved.reshape(-1, 128)


def on_device(pair_rep, side_weight, gate_weight, out_weight, in_gain, out_gain):
    pair = pair_rep.reshape(PAIR[0])
    side_weight = side_weight.reshape(8, 128, 128)
    sides, gate, gains = call(
        project_kernel,
        [SIDES, GATE, GAIN],
        [PAIR, ((4, 128, 128), BF16), ((128, 128), BF16), *PROJECT_SCRATCH, pltpu.SemaphoreType.DMA((5,))],
        pair, side_weight, gate_weight, in_gain, out_gain,
        hbm=range(5),
    )
    regroup = jnp.asarray(np.eye(512).reshape(4, 4, 32, 512).transpose(1, 0, 2, 3).reshape(512, 512).T, BF16)
    finish_scratch = [((16, 128, 128), F32)]
    for update in range(2):
        sides = exchange(sides)
        triangle = functools.partial(triangle_kernel, update=update)
        (mixed,) = call(triangle, [MIXED], [((512, 512), BF16)] * 2, sides, regroup)
        mixed = exchange(mixed)
        finish = functools.partial(finish_kernel, update=update)
        operands = (mixed, pair, gate, out_weight, gains)
        if update == 0:
            pair, sides, gate = call(
                finish, [PAIR, SIDES, GATE], finish_scratch + PROJECT_SCRATCH,
                *operands, side_weight, gate_weight,
            )
        else:
            scratch = [((3072, 128), F32), PAIR, pltpu.SemaphoreType.DMA((4,))]
            (pair,) = call(finish, [((4, 16, 32, 128), BF16)], scratch, *operands, hbm_out=True)
    return pair.reshape(pair_rep.shape)


def solution(mesh):
    physical = jax.sharding.Mesh(mesh.devices.reshape((2,) * 7), BITS)
    tile = P(BITS[:3], BITS[3:], None)
    return jax.shard_map(
        on_device, mesh=physical, in_specs=(tile, P(), P(), P(), P(), P()), out_specs=tile, check_vma=False
    )
```

```python
import functools

import jax
import jax.numpy as jnp
import numpy as np
from jax import lax
from jax.experimental import pallas as pl
from jax.experimental.pallas import tpu as pltpu
from jax.sharding import PartitionSpec as P

epsilon = 1e-05
F32 = jnp.float32
BF16 = jnp.bfloat16

BITS = ("y_hi", "y_lo", "z_lo", "x_hi", "x_lo", "z_hi", "core")
ORDER = BITS


def device_number(r, c):
    return 16 * r + c


def dot(a, b, dims):
    return lax.dot_general(a, b, (dims, ((), ())), preferred_element_type=F32)


def ahead(items, produce, consume):
    waiting = None
    for item in items:
        made = produce(item)
        if waiting is not None:
            consume(*waiting)
        waiting = (item, made)
    consume(*waiting)


def two_blocks(matrix):
    zero = jnp.zeros_like(matrix)
    return jnp.concatenate(
        [jnp.concatenate([matrix, zero], axis=1), jnp.concatenate([zero, matrix], axis=1)], axis=0
    )


def side_by_side(ref, n):
    return jnp.concatenate([ref[n : n + 512, :], ref[n + 512 : n + 1024, :]], axis=1)


def norm_rows(pair_ref, arrive, gain, centred_ref, normed_ref):
    row = lax.broadcasted_iota(jnp.int32, (128, 128), 0)
    column = lax.broadcasted_iota(jnp.int32, (128, 128), 1)
    centring = two_blocks(jnp.where(row == column, 127.0 / 128.0, -1.0 / 128.0).astype(BF16))
    average = two_blocks(jnp.full((128, 128), 1.0 / 128.0, BF16))
    for n in range(0, 2048, 1024):
        arrive(n)
        centred_ref[n // 2 : n // 2 + 512, :] = dot(side_by_side(pair_ref, n), centring, ((1,), (0,)))

    gains = jnp.concatenate([gain(), gain()], axis=1)

    def spread(n):
        centred = centred_ref[n // 2 : n // 2 + 512, :]
        return dot((centred * centred).astype(BF16), average, ((1,), (0,)))

    def scale(n, variance):
        normed = (centred_ref[n // 2 : n // 2 + 512, :] * lax.rsqrt(variance + epsilon) * gains).astype(BF16)
        normed_ref[n : n + 512, :] = normed[:, :128]
        normed_ref[n + 512 : n + 1024, :] = normed[:, 128:]

    ahead(range(0, 2048, 1024), spread, scale)


def project(pair_ref, arrive, gain, wt_ref, gate_weight, refs, out_ref, gate_ref):
    centred_ref, normed_ref, half_ref = refs
    norm_rows(pair_ref, arrive, gain, centred_ref, normed_ref)
    slabs = normed_ref.reshape(4, 16, 32, 128)
    def product(place):
        s, side = place
        normed = jnp.concatenate([slabs[:, s + n].reshape(128, 128) for n in range(2)], axis=0)
        return dot(wt_ref[256 * side : 256 * side + 256], normed, ((1,), (1,))).reshape(16, 2, 8, 256)

    def gated(place, both):
        s, side = place
        result = (both[:, 0] + both[:, 0] * jnp.tanh(both[:, 1])).reshape(128, 256)
        for n in range(2):
            half_ref[pl.ds(side * 16 + s + n, 128, stride=40), :] = result[:, 128 * n : 128 * n + 128]

    ahead([(s, side) for s in range(0, 16, 2) for side in range(2)], product, gated)
    weight = two_blocks(halved(gate_weight()))

    def gate_product(n):
        return dot(side_by_side(normed_ref, n), weight, ((1,), (0,)))

    def gate(n, values):
        values = jnp.tanh(values)
        gate_ref[n : n + 512, :] = values[:, :128]
        gate_ref[n + 512 : n + 1024, :] = values[:, 128:]

    ahead(range(0, 2048, 1024), gate_product, gate)
    for channel in range(0, 128, 16):
        part = half_ref[channel * 40 : channel * 40 + 640, :].reshape(16, 40, 128)[:, :32]
        out_ref[channel : channel + 16] = part.astype(BF16).reshape(16, 2, 16, 128)


def halved(weight):
    return (0.5 * weight.astype(F32)).astype(BF16)


def fill_weights(side_ref, wt_ref, update):
    for side in range(2):
        value, gate = [
            (0.5 * side_ref[4 * update + 2 * side + n].astype(F32)).T.reshape(16, 1, 8, 128) for n in range(2)
        ]
        both = jnp.concatenate([value, gate], axis=1).reshape(256, 128)
        wt_ref[256 * side : 256 * side + 256, :] = both.astype(BF16)


def project_kernel(
    pair_hbm, side_hbm, gate_weight_hbm, gain_hbm, out_gain_hbm, out_ref, gate_ref, gain_ref, pair_ref, side_ref, gate_weight_ref,
    wt_ref, centred_ref, normed_ref, half_ref, sems,
):
    halves = [pl.ds(n, 1024) for n in (0, 1024)]
    copies = [
        *[pltpu.make_async_copy(pair_hbm.at[half], pair_ref.at[half], sems.at[n]) for n, half in enumerate(halves)],
        pltpu.make_async_copy(side_hbm.at[pl.ds(0, 4)], side_ref, sems.at[2]),
        pltpu.make_async_copy(gate_weight_hbm.at[0], gate_weight_ref, sems.at[3]),
        pltpu.make_async_copy(gain_hbm, gain_ref.at[0], sems.at[4]),
        pltpu.make_async_copy(out_gain_hbm, gain_ref.at[1], sems.at[5]),
    ]
    for copy in copies:
        copy.start()

    def arrive(n):
        if n == 0:
            copies[0].wait()
        else:
            for copy in copies[1:]:
                copy.wait()
            fill_weights(side_ref, wt_ref, 0)

    project(
        pair_ref, arrive, lambda: gain_ref[0, 0:1, :], wt_ref, lambda: gate_weight_ref[...],
        (centred_ref, normed_ref, half_ref), out_ref, gate_ref,
    )


def swap_groups(groups, low, even):
    halves = [pair for t in groups for pair in ((t[0], t[2]), (t[1], t[3]))]
    moved = [pltpu.roll(jnp.where(low, b, a), 64, 1) for a, b in halves]
    halves = [(jnp.where(low, a, m), jnp.where(low, m, b)) for (a, b), m in zip(halves, moved)]
    crossed = []
    for (u0, u2), (u1, u3) in zip(halves[::2], halves[1::2]):
        crossed += [(u0, u1), (u2, u3)]
    rolled = [(pltpu.roll(b, 32, 1), pltpu.roll(a, 96, 1)) for a, b in crossed]
    out = [
        (jnp.where(even, a, to_first), jnp.where(even, to_second, b))
        for (a, b), (to_first, to_second) in zip(crossed, rolled)
    ]
    return [first + second for first, second in zip(out[::2], out[1::2])]


def triangle_kernel(in_ref, regroup_ref, out_ref, left_ref, right_ref, *, update):
    lane = lax.broadcasted_iota(jnp.int32, (16, 128), 1)
    low = lane < 64
    even = (lane & 32) == 0


    def stacked(side, places):
        tiles = []
        for n in range(4):
            numbers = [device_number(r, 4 * block + n) for r, block in places]
            tiles.append(jnp.concatenate([in_ref[32 * m + 16 * side : 32 * m + 16 * side + 16, :] for m in numbers], axis=0))
        return jnp.concatenate(tiles, axis=1)

    for half in range(2):
        if update == 0:
            places = [(4 * half + r, block) for r in range(4) for block in range(4)]
            regrouped = dot(stacked(1, places), regroup_ref[...], ((1,), (0,))).astype(BF16)
            for m, (r, block) in enumerate(places):
                for g in range(4):
                    row = r * 64 + g * 16
                    tile = regrouped[16 * m : 16 * m + 16, 128 * g : 128 * g + 128]
                    right_ref[row : row + 16, 128 * block : 128 * block + 128] = tile
        else:
            places = [(r, 2 * half + block) for block in range(2) for r in range(8)]
            regrouped = dot(regroup_ref[...], stacked(0, places), ((1,), (1,))).astype(BF16)
            for block in range(2):
                for g in range(4):
                    row = 128 * (2 * half + block)
                    tile = regrouped[128 * g : 128 * g + 128, 128 * block : 128 * block + 128]
                    left_ref[row : row + 128, 128 * g : 128 * g + 128] = tile
    side, full_ref = ((0, left_ref), (1, right_ref))[update]
    places = [(r, block) for r in range(8) for block in range(4)]
    groups = []
    for r, block in places:
        numbers = [device_number(r, 4 * block + n) for n in range(4)]
        groups.append([in_ref[32 * m + 16 * side : 32 * m + 16 * side + 16, :] for m in numbers])
    for (r, block), tiles in zip(places, swap_groups(groups, low, even)):
        for g, tile in enumerate(tiles):
            row = r * 64 + g * 16 if update == 0 else g * 128 + r * 16
            full_ref[row : row + 16, 128 * block : 128 * block + 128] = tile
    products = []
    for half in range(2):
        part = slice(256 * half, 256 * half + 256)
        if update == 0:
            products.append(dot(left_ref[...], right_ref[part, :], ((1,), (1,))).astype(BF16))
        else:
            products.append(dot(left_ref[...], right_ref[:, part], ((1,), (0,))).astype(BF16))
    for half, mixed in enumerate(products):
        places = [(r, block) for r in range(8) for block in range(2)]
        groups = [
            [mixed[r * 64 + 16 * g : r * 64 + 16 * g + 16, 128 * block : 128 * block + 128] for g in range(4)]
            for r, block in places
        ]
        for (r, block), tiles in zip(places, swap_groups(groups, low, even)):
            for n, tile in enumerate(tiles):
                row = device_number(r, 8 * half + 4 * block + n) * 16
                out_ref[row : row + 16, :] = tile


def finish_kernel(mixed_ref, pair_ref, gate_ref, out_weight_ref, gain_ref, *rest, update):
    if update == 0:
        (side_ref, gate_weight_ref, pair_out_ref, out_ref, gate_out_ref, raw_ref, wt_ref, centred_ref,
         normed_ref, half_ref) = rest
    else:
        pair_hbm, raw_ref, pair_out_ref, sems = rest
    if update == 0:
        fill_weights(side_ref, wt_ref, 1)
    for channel in range(0, 128, 16):
        part = mixed_ref[16 * channel : 16 * channel + 256, :].astype(F32).reshape(16, 16, 128)
        for n in range(16):
            raw_ref[24 * (channel + n) : 24 * (channel + n) + 16, :] = part[n]
    out_gain = jnp.broadcast_to(gain_ref[1, update : update + 1, :], (128, 128)).T
    weight = two_blocks(halved(out_weight_ref[update]))
    slabs = [ref.reshape(4, 16, 32, 128) for ref in (pair_ref, gate_ref, pair_out_ref)]
    copies = []
    out_normed = {}
    for s in range(0, 18, 2):
        if s < 16:
            values = jnp.stack([raw_ref[pl.ds(s + n, 128, stride=24), :] for n in range(2)])
            centred = values - jnp.mean(values, axis=1, keepdims=True)
            variance = jnp.mean(centred * centred, axis=1, keepdims=True)
            out_normed[s] = (centred * lax.rsqrt(variance + epsilon) * out_gain).astype(BF16)
        if s == 0:
            continue
        changes = dot(out_normed[s - 2].reshape(256, 128), weight, ((0,), (0,)))
        for n in range(2):
            change = changes[:, 128 * n : 128 * n + 128].reshape(4, 32, 128)
            before, gate = slabs[0][:, s - 2 + n].astype(F32), slabs[1][:, s - 2 + n]
            slabs[2][:, s - 2 + n] = (before + (change + change * gate)).astype(BF16)
        if update == 1 and s % 4 == 0:
            part = pl.ds(s - 4, 4)
            copies.append(pltpu.make_async_copy(slabs[2].at[:, part], pair_hbm.at[:, part], sems.at[s // 4 - 1]))
            copies[-1].start()
    for copy in copies:
        copy.wait()
    if update == 0:
        project(
            pair_out_ref, lambda n: None, lambda: gain_ref[0, 1:2, :], wt_ref, lambda: gate_weight_ref[1],
            (centred_ref, normed_ref, half_ref), out_ref, gate_out_ref,
        )


def call(kernel, out, scratch, *operands, hbm=(), hbm_out=False):
    operands = [pltpu.with_memory_space_constraint(a, pltpu.HBM) if n in hbm else a for n, a in enumerate(operands)]
    spaces = [pltpu.HBM if n in hbm else pltpu.VMEM for n in range(len(operands))]
    return pl.pallas_call(
        kernel,
        out_shape=[jax.ShapeDtypeStruct(*one) for one in out],
        in_specs=[pl.BlockSpec(memory_space=space) for space in spaces],
        out_specs=[pl.BlockSpec(memory_space=pltpu.HBM if hbm_out else pltpu.VMEM) for _ in out],
        scratch_shapes=[pltpu.VMEM(*one) if isinstance(one, tuple) else one for one in scratch],
        compiler_params=pltpu.CompilerParams(vmem_limit_bytes=32 * 1024 * 1024),
    )(*operands)


SIDES = ((128, 2, 16, 128), BF16)
MIXED = ((2048, 128), BF16)
PAIR = ((2048, 128), BF16)
GATE = ((2048, 128), F32)
GAIN = ((2, 2, 128), F32)
PROJECT_SCRATCH = [((512, 128), BF16), ((1024, 256), F32), ((2048, 128), BF16), ((5120, 128), F32)]


def exchange(flat):
    pieces = flat.reshape(128, -1, 128)
    moved = lax.all_to_all(pieces, ORDER, split_axis=0, concat_axis=0, tiled=True)
    return moved.reshape(-1, 128)


def on_device(pair_rep, side_weight, gate_weight, out_weight, in_gain, out_gain):
    pair = pair_rep.reshape(PAIR[0])
    side_weight = side_weight.reshape(8, 128, 128)
    sides, gate, gains = call(
        project_kernel,
        [SIDES, GATE, GAIN],
        [PAIR, ((4, 128, 128), BF16), ((128, 128), BF16), *PROJECT_SCRATCH, pltpu.SemaphoreType.DMA((6,))],
        pair, side_weight, gate_weight, in_gain, out_gain,
        hbm=range(5),
    )
    regroup = jnp.asarray(np.eye(512).reshape(4, 4, 32, 512).transpose(1, 0, 2, 3).reshape(512, 512).T, BF16)
    finish_scratch = [((3072, 128), F32)]
    for update in range(2):
        sides = exchange(sides)
        triangle = functools.partial(triangle_kernel, update=update)
        (mixed,) = call(triangle, [MIXED], [((512, 512), BF16)] * 2, sides, regroup)
        mixed = exchange(mixed)
        finish = functools.partial(finish_kernel, update=update)
        operands = (mixed, pair, gate, out_weight, gains)
        if update == 0:
            pair, sides, gate = call(
                finish, [PAIR, SIDES, GATE], finish_scratch + PROJECT_SCRATCH,
                *operands, side_weight, gate_weight,
            )
        else:
            scratch = finish_scratch + [PAIR, pltpu.SemaphoreType.DMA((4,))]
            (pair,) = call(finish, [((4, 16, 32, 128), BF16)], scratch, *operands, hbm_out=True)
    return pair.reshape(pair_rep.shape)


def solution(mesh):
    physical = jax.sharding.Mesh(mesh.devices.reshape((2,) * 7), BITS)
    tile = P(BITS[:3], BITS[3:], None)
    return jax.shard_map(
        on_device, mesh=physical, in_specs=(tile, P(), P(), P(), P(), P()), out_specs=tile, check_vma=False
    )
```

```python
import functools

import jax
import jax.numpy as jnp
import numpy as np
from jax import lax
from jax.experimental import pallas as pl
from jax.experimental.pallas import tpu as pltpu
from jax.sharding import PartitionSpec as P

epsilon = 1e-05
F32 = jnp.float32
BF16 = jnp.bfloat16

BITS = ("y_hi", "y_lo", "z_lo", "x_hi", "x_lo", "z_hi", "core")
ORDER = BITS


def device_number(r, c):
    return 16 * r + c


def dot(a, b, dims):
    return lax.dot_general(a, b, (dims, ((), ())), preferred_element_type=F32)


def ahead(items, produce, consume):
    waiting = None
    for item in items:
        made = produce(item)
        if waiting is not None:
            consume(*waiting)
        waiting = (item, made)
    consume(*waiting)


def two_blocks(matrix):
    zero = jnp.zeros_like(matrix)
    return jnp.concatenate(
        [jnp.concatenate([matrix, zero], axis=1), jnp.concatenate([zero, matrix], axis=1)], axis=0
    )


def side_by_side(ref, n):
    return jnp.concatenate([ref[n : n + 512, :], ref[n + 512 : n + 1024, :]], axis=1)


def norm_rows(pair_ref, gain, centred_ref, normed_ref, lanes):
    row = lax.broadcasted_iota(jnp.int32, (128, 128), 0)
    column = lax.broadcasted_iota(jnp.int32, (128, 128), 1)
    centring = two_blocks(jnp.where(row == column, 127.0 / 128.0, -1.0 / 128.0).astype(BF16))
    average = two_blocks(jnp.full((128, 128), 1.0 / 128.0, BF16))
    for n in range(0, 2048, 1024):
        if lanes:
            for m in range(2):
                values = pair_ref[n + 512 * m : n + 512 * m + 512, :].astype(F32)
                centred = values - jnp.mean(values, axis=1, keepdims=True)
                centred_ref[n // 2 : n // 2 + 512, 128 * m : 128 * m + 128] = centred
        else:
            centred_ref[n // 2 : n // 2 + 512, :] = dot(side_by_side(pair_ref, n), centring, ((1,), (0,)))
    gains = jnp.concatenate([gain, gain], axis=1)

    def spread(n):
        centred = centred_ref[n // 2 : n // 2 + 512, :]
        return dot((centred * centred).astype(BF16), average, ((1,), (0,)))

    def scale(n, variance):
        normed = (centred_ref[n // 2 : n // 2 + 512, :] * lax.rsqrt(variance + epsilon) * gains).astype(BF16)
        normed_ref[n : n + 512, :] = normed[:, :128]
        normed_ref[n + 512 : n + 1024, :] = normed[:, 128:]

    ahead(range(0, 2048, 1024), spread, scale)


def project(pair_ref, gain, wt_ref, gate_weight, refs, out_ref, gate_ref, lanes=False):
    centred_ref, normed_ref, half_ref = refs
    norm_rows(pair_ref, gain, centred_ref, normed_ref, lanes)
    slabs = normed_ref.reshape(4, 16, 32, 128)
    def product(place):
        s, side = place
        normed = jnp.concatenate([slabs[:, s + n].reshape(128, 128) for n in range(2)], axis=0)
        return dot(wt_ref[256 * side : 256 * side + 256], normed, ((1,), (1,))).reshape(16, 2, 8, 256)

    def gated(place, both):
        s, side = place
        result = (both[:, 0] + both[:, 0] * jnp.tanh(both[:, 1])).reshape(128, 256)
        for n in range(2):
            half_ref[pl.ds(side * 16 + s + n, 128, stride=40), :] = result[:, 128 * n : 128 * n + 128]

    ahead([(s, side) for s in range(0, 16, 2) for side in range(2)], product, gated)
    weight = two_blocks(halved(gate_weight))

    def gate_product(n):
        return dot(side_by_side(normed_ref, n), weight, ((1,), (0,)))

    def gate(n, values):
        values = jnp.tanh(values)
        gate_ref[n : n + 512, :] = values[:, :128]
        gate_ref[n + 512 : n + 1024, :] = values[:, 128:]

    ahead(range(0, 2048, 1024), gate_product, gate)
    for channel in range(0, 128, 16):
        part = half_ref[channel * 40 : channel * 40 + 640, :].reshape(16, 40, 128)[:, :32]
        out_ref[channel : channel + 16] = part.astype(BF16).reshape(16, 2, 16, 128)


def halved(weight):
    return (0.5 * weight.astype(F32)).astype(BF16)


def fill_weights(side_ref, wt_ref, update):
    for side in range(2):
        value, gate = [
            (0.5 * side_ref[4 * update + 2 * side + n].astype(F32)).T.reshape(16, 1, 8, 128) for n in range(2)
        ]
        both = jnp.concatenate([value, gate], axis=1).reshape(256, 128)
        wt_ref[256 * side : 256 * side + 256, :] = both.astype(BF16)


def project_kernel(
    pair_hbm, side_hbm, gate_weight_hbm, gain_hbm, out_gain_hbm, out_ref, gate_ref, gain_ref, pair_ref, side_ref, gate_weight_ref,
    wt_ref, centred_ref, normed_ref, half_ref, sems,
):
    copies = [
        pltpu.make_async_copy(side_hbm.at[pl.ds(0, 4)], side_ref, sems.at[0]),
        pltpu.make_async_copy(pair_hbm, pair_ref, sems.at[1]),
        pltpu.make_async_copy(gate_weight_hbm.at[0], gate_weight_ref, sems.at[2]),
        pltpu.make_async_copy(gain_hbm, gain_ref.at[0], sems.at[3]),
        pltpu.make_async_copy(out_gain_hbm, gain_ref.at[1], sems.at[4]),
    ]
    for copy in copies:
        copy.start()
    copies[0].wait()
    fill_weights(side_ref, wt_ref, 0)
    for copy in copies[1:]:
        copy.wait()
    project(
        pair_ref, gain_ref[0, 0:1, :], wt_ref, gate_weight_ref[...],
        (centred_ref, normed_ref, half_ref), out_ref, gate_ref, True,
    )


def swap_groups(groups, low, even):
    halves = [pair for t in groups for pair in ((t[0], t[2]), (t[1], t[3]))]
    moved = [pltpu.roll(jnp.where(low, b, a), 64, 1) for a, b in halves]
    halves = [(jnp.where(low, a, m), jnp.where(low, m, b)) for (a, b), m in zip(halves, moved)]
    crossed = []
    for (u0, u2), (u1, u3) in zip(halves[::2], halves[1::2]):
        crossed += [(u0, u1), (u2, u3)]
    rolled = [(pltpu.roll(b, 32, 1), pltpu.roll(a, 96, 1)) for a, b in crossed]
    out = [
        (jnp.where(even, a, to_first), jnp.where(even, to_second, b))
        for (a, b), (to_first, to_second) in zip(crossed, rolled)
    ]
    return [first + second for first, second in zip(out[::2], out[1::2])]


def triangle_kernel(in_ref, regroup_ref, out_ref, left_ref, right_ref, *, update):
    lane = lax.broadcasted_iota(jnp.int32, (16, 128), 1)
    low = lane < 64
    even = (lane & 32) == 0


    def stacked(side, places):
        tiles = []
        for n in range(4):
            numbers = [device_number(r, 4 * block + n) for r, block in places]
            tiles.append(jnp.concatenate([in_ref[32 * m + 16 * side : 32 * m + 16 * side + 16, :] for m in numbers], axis=0))
        return jnp.concatenate(tiles, axis=1)

    for half in range(2):
        if update == 0:
            places = [(4 * half + r, block) for r in range(4) for block in range(4)]
            regrouped = dot(stacked(1, places), regroup_ref[...], ((1,), (0,))).astype(BF16)
            for m, (r, block) in enumerate(places):
                for g in range(4):
                    row = r * 64 + g * 16
                    tile = regrouped[16 * m : 16 * m + 16, 128 * g : 128 * g + 128]
                    right_ref[row : row + 16, 128 * block : 128 * block + 128] = tile
        else:
            places = [(r, 2 * half + block) for block in range(2) for r in range(8)]
            regrouped = dot(regroup_ref[...], stacked(0, places), ((1,), (1,))).astype(BF16)
            for block in range(2):
                for g in range(4):
                    row = 128 * (2 * half + block)
                    tile = regrouped[128 * g : 128 * g + 128, 128 * block : 128 * block + 128]
                    left_ref[row : row + 128, 128 * g : 128 * g + 128] = tile
    side, full_ref = ((0, left_ref), (1, right_ref))[update]
    places = [(r, block) for r in range(8) for block in range(4)]
    groups = []
    for r, block in places:
        numbers = [device_number(r, 4 * block + n) for n in range(4)]
        groups.append([in_ref[32 * m + 16 * side : 32 * m + 16 * side + 16, :] for m in numbers])
    for (r, block), tiles in zip(places, swap_groups(groups, low, even)):
        for g, tile in enumerate(tiles):
            row = r * 64 + g * 16 if update == 0 else g * 128 + r * 16
            full_ref[row : row + 16, 128 * block : 128 * block + 128] = tile
    products = []
    for half in range(2):
        part = slice(256 * half, 256 * half + 256)
        if update == 0:
            products.append(dot(left_ref[...], right_ref[part, :], ((1,), (1,))).astype(BF16))
        else:
            products.append(dot(left_ref[...], right_ref[:, part], ((1,), (0,))).astype(BF16))
    for half, mixed in enumerate(products):
        places = [(r, block) for r in range(8) for block in range(2)]
        groups = [
            [mixed[r * 64 + 16 * g : r * 64 + 16 * g + 16, 128 * block : 128 * block + 128] for g in range(4)]
            for r, block in places
        ]
        for (r, block), tiles in zip(places, swap_groups(groups, low, even)):
            for n, tile in enumerate(tiles):
                row = device_number(r, 8 * half + 4 * block + n) * 16
                out_ref[row : row + 16, :] = tile


def finish_kernel(mixed_ref, pair_ref, gate_ref, out_weight_ref, gain_ref, *rest, update):
    if update == 0:
        (side_ref, gate_weight_ref, pair_out_ref, out_ref, gate_out_ref, raw_ref, wt_ref, centred_ref,
         normed_ref, half_ref) = rest
    else:
        pair_hbm, raw_ref, pair_out_ref, sems = rest
    if update == 0:
        fill_weights(side_ref, wt_ref, 1)
    for channel in range(0, 128, 16):
        part = mixed_ref[16 * channel : 16 * channel + 256, :].astype(F32).reshape(16, 16, 128)
        for n in range(16):
            raw_ref[24 * (channel + n) : 24 * (channel + n) + 16, :] = part[n]
    out_gain = jnp.broadcast_to(gain_ref[1, update : update + 1, :], (128, 128)).T
    weight = two_blocks(halved(out_weight_ref[update]))
    slabs = [ref.reshape(4, 16, 32, 128) for ref in (pair_ref, gate_ref, pair_out_ref)]
    copies = []
    out_normed = {}
    for s in range(0, 18, 2):
        if s < 16:
            values = jnp.stack([raw_ref[pl.ds(s + n, 128, stride=24), :] for n in range(2)])
            centred = values - jnp.mean(values, axis=1, keepdims=True)
            variance = jnp.mean(centred * centred, axis=1, keepdims=True)
            out_normed[s] = (centred * lax.rsqrt(variance + epsilon) * out_gain).astype(BF16)
        if s == 0:
            continue
        changes = dot(out_normed[s - 2].reshape(256, 128), weight, ((0,), (0,)))
        for n in range(2):
            change = changes[:, 128 * n : 128 * n + 128].reshape(4, 32, 128)
            before, gate = slabs[0][:, s - 2 + n].astype(F32), slabs[1][:, s - 2 + n]
            slabs[2][:, s - 2 + n] = (before + (change + change * gate)).astype(BF16)
        if update == 1 and s % 4 == 0:
            part = pl.ds(s - 4, 4)
            copies.append(pltpu.make_async_copy(slabs[2].at[:, part], pair_hbm.at[:, part], sems.at[s // 4 - 1]))
            copies[-1].start()
    for copy in copies:
        copy.wait()
    if update == 0:
        project(
            pair_out_ref, gain_ref[0, 1:2, :], wt_ref, gate_weight_ref[1],
            (centred_ref, normed_ref, half_ref), out_ref, gate_out_ref,
        )


def call(kernel, out, scratch, *operands, hbm=(), hbm_out=False):
    operands = [pltpu.with_memory_space_constraint(a, pltpu.HBM) if n in hbm else a for n, a in enumerate(operands)]
    spaces = [pltpu.HBM if n in hbm else pltpu.VMEM for n in range(len(operands))]
    return pl.pallas_call(
        kernel,
        out_shape=[jax.ShapeDtypeStruct(*one) for one in out],
        in_specs=[pl.BlockSpec(memory_space=space) for space in spaces],
        out_specs=[pl.BlockSpec(memory_space=pltpu.HBM if hbm_out else pltpu.VMEM) for _ in out],
        scratch_shapes=[pltpu.VMEM(*one) if isinstance(one, tuple) else one for one in scratch],
        compiler_params=pltpu.CompilerParams(vmem_limit_bytes=32 * 1024 * 1024),
    )(*operands)


SIDES = ((128, 2, 16, 128), BF16)
MIXED = ((2048, 128), BF16)
PAIR = ((2048, 128), BF16)
GATE = ((2048, 128), F32)
GAIN = ((2, 2, 128), F32)
PROJECT_SCRATCH = [((512, 128), BF16), ((1024, 256), F32), ((2048, 128), BF16), ((5120, 128), F32)]


def exchange(flat):
    pieces = flat.reshape(128, -1, 128)
    moved = lax.all_to_all(pieces, ORDER, split_axis=0, concat_axis=0, tiled=True)
    return moved.reshape(-1, 128)


def on_device(pair_rep, side_weight, gate_weight, out_weight, in_gain, out_gain):
    pair = pair_rep.reshape(PAIR[0])
    side_weight = side_weight.reshape(8, 128, 128)
    sides, gate, gains = call(
        project_kernel,
        [SIDES, GATE, GAIN],
        [PAIR, ((4, 128, 128), BF16), ((128, 128), BF16), *PROJECT_SCRATCH, pltpu.SemaphoreType.DMA((5,))],
        pair, side_weight, gate_weight, in_gain, out_gain,
        hbm=range(5),
    )
    regroup = jnp.asarray(np.eye(512).reshape(4, 4, 32, 512).transpose(1, 0, 2, 3).reshape(512, 512).T, BF16)
    finish_scratch = [((3072, 128), F32)]
    for update in range(2):
        sides = exchange(sides)
        triangle = functools.partial(triangle_kernel, update=update)
        (mixed,) = call(triangle, [MIXED], [((512, 512), BF16)] * 2, sides, regroup)
        mixed = exchange(mixed)
        finish = functools.partial(finish_kernel, update=update)
        operands = (mixed, pair, gate, out_weight, gains)
        if update == 0:
            pair, sides, gate = call(
                finish, [PAIR, SIDES, GATE], finish_scratch + PROJECT_SCRATCH,
                *operands, side_weight, gate_weight,
            )
        else:
            scratch = finish_scratch + [PAIR, pltpu.SemaphoreType.DMA((4,))]
            (pair,) = call(finish, [((4, 16, 32, 128), BF16)], scratch, *operands, hbm_out=True)
    return pair.reshape(pair_rep.shape)


def solution(mesh):
    physical = jax.sharding.Mesh(mesh.devices.reshape((2,) * 7), BITS)
    tile = P(BITS[:3], BITS[3:], None)
    return jax.shard_map(
        on_device, mesh=physical, in_specs=(tile, P(), P(), P(), P(), P()), out_specs=tile, check_vma=False
    )
```

```python
import functools

import jax
import jax.numpy as jnp
import numpy as np
from jax import lax
from jax.experimental import pallas as pl
from jax.experimental.pallas import tpu as pltpu
from jax.sharding import PartitionSpec as P

epsilon = 1e-05
F32 = jnp.float32
BF16 = jnp.bfloat16

BITS = ("y_hi", "y_lo", "z_lo", "x_hi", "x_lo", "z_hi", "core")
ORDER = BITS


def device_number(r, c):
    return 16 * r + c


def dot(a, b, dims):
    return lax.dot_general(a, b, (dims, ((), ())), preferred_element_type=F32)


def ahead(items, produce, consume):
    waiting = None
    for item in items:
        made = produce(item)
        if waiting is not None:
            consume(*waiting)
        waiting = (item, made)
    consume(*waiting)


def two_blocks(matrix):
    zero = jnp.zeros_like(matrix)
    return jnp.concatenate(
        [jnp.concatenate([matrix, zero], axis=1), jnp.concatenate([zero, matrix], axis=1)], axis=0
    )


def side_by_side(ref, n):
    return jnp.concatenate([ref[n : n + 512, :], ref[n + 512 : n + 1024, :]], axis=1)


def norm_rows(pair_ref, gain, centred_ref, normed_ref, lanes):
    average = two_blocks(jnp.full((128, 128), 1.0 / 128.0, BF16))
    for n in range(0, 2048, 512):
        values = pair_ref[n : n + 512, :].astype(F32)
        row, lane = n // 1024 * 512, n % 1024 // 512 * 128
        centred_ref[row : row + 512, lane : lane + 128] = values - jnp.mean(values, axis=1, keepdims=True)
    gains = jnp.concatenate([gain, gain], axis=1)

    def spread(n):
        centred = centred_ref[n // 2 : n // 2 + 512, :]
        square = centred * centred
        if lanes:
            return [jnp.mean(square[:, m : m + 128], axis=1, keepdims=True) for m in (0, 128)]
        return dot(square.astype(BF16), average, ((1,), (0,)))

    def scale(n, variance):
        if lanes:
            for m in range(2):
                centred = centred_ref[n // 2 : n // 2 + 512, 128 * m : 128 * m + 128]
                normed = (centred * lax.rsqrt(variance[m] + epsilon) * gain).astype(BF16)
                normed_ref[n + 512 * m : n + 512 * m + 512, :] = normed
            return
        normed = (centred_ref[n // 2 : n // 2 + 512, :] * lax.rsqrt(variance + epsilon) * gains).astype(BF16)
        normed_ref[n : n + 512, :] = normed[:, :128]
        normed_ref[n + 512 : n + 1024, :] = normed[:, 128:]

    ahead(range(0, 2048, 1024), spread, scale)


def project(pair_ref, gain, wt_ref, gate_weight, refs, out_ref, gate_ref, lanes):
    centred_ref, normed_ref, half_ref = refs
    norm_rows(pair_ref, gain, centred_ref, normed_ref, lanes)
    slabs = normed_ref.reshape(4, 16, 32, 128)
    def product(place):
        s, side = place
        normed = jnp.concatenate([slabs[:, s + n].reshape(128, 128) for n in range(2)], axis=0)
        return dot(wt_ref[256 * side : 256 * side + 256], normed, ((1,), (1,))).reshape(16, 2, 8, 256)

    def gated(place, both):
        s, side = place
        result = (both[:, 0] + both[:, 0] * jnp.tanh(both[:, 1])).reshape(128, 256)
        for n in range(2):
            half_ref[pl.ds(side * 16 + s + n, 128, stride=40), :] = result[:, 128 * n : 128 * n + 128]

    ahead([(s, side) for s in range(0, 16, 2) for side in range(2)], product, gated)
    weight = two_blocks(halved(gate_weight))

    def gate_product(n):
        return dot(side_by_side(normed_ref, n), weight, ((1,), (0,)))

    def gate(n, values):
        values = jnp.tanh(values)
        gate_ref[n : n + 512, :] = values[:, :128]
        gate_ref[n + 512 : n + 1024, :] = values[:, 128:]

    ahead(range(0, 2048, 1024), gate_product, gate)
    for channel in range(0, 128, 16):
        part = half_ref[channel * 40 : channel * 40 + 640, :].reshape(16, 40, 128)[:, :32]
        out_ref[channel : channel + 16] = part.astype(BF16).reshape(16, 2, 16, 128)


def halved(weight):
    return (0.5 * weight.astype(F32)).astype(BF16)


def fill_weights(side_ref, wt_ref, update):
    for side in range(2):
        value, gate = [
            (0.5 * side_ref[4 * update + 2 * side + n].astype(F32)).T.reshape(16, 1, 8, 128) for n in range(2)
        ]
        both = jnp.concatenate([value, gate], axis=1).reshape(256, 128)
        wt_ref[256 * side : 256 * side + 256, :] = both.astype(BF16)


def project_kernel(
    pair_hbm, side_hbm, gate_weight_hbm, gain_hbm, out_gain_hbm, out_ref, gate_ref, gain_ref, pair_ref, side_ref, gate_weight_ref,
    wt_ref, centred_ref, normed_ref, half_ref, sems,
):
    copies = [
        pltpu.make_async_copy(side_hbm.at[pl.ds(0, 4)], side_ref, sems.at[0]),
        pltpu.make_async_copy(pair_hbm, pair_ref, sems.at[1]),
        pltpu.make_async_copy(gate_weight_hbm.at[0], gate_weight_ref, sems.at[2]),
        pltpu.make_async_copy(gain_hbm, gain_ref.at[0], sems.at[3]),
        pltpu.make_async_copy(out_gain_hbm, gain_ref.at[1], sems.at[4]),
    ]
    for copy in copies:
        copy.start()
    copies[0].wait()
    fill_weights(side_ref, wt_ref, 0)
    for copy in copies[1:]:
        copy.wait()
    project(
        pair_ref, gain_ref[0, 0:1, :], wt_ref, gate_weight_ref[...],
        (centred_ref, normed_ref, half_ref), out_ref, gate_ref, False,
    )


def swap_groups(groups, low, even):
    halves = [pair for t in groups for pair in ((t[0], t[2]), (t[1], t[3]))]
    moved = [pltpu.roll(jnp.where(low, b, a), 64, 1) for a, b in halves]
    halves = [(jnp.where(low, a, m), jnp.where(low, m, b)) for (a, b), m in zip(halves, moved)]
    crossed = []
    for (u0, u2), (u1, u3) in zip(halves[::2], halves[1::2]):
        crossed += [(u0, u1), (u2, u3)]
    rolled = [(pltpu.roll(b, 32, 1), pltpu.roll(a, 96, 1)) for a, b in crossed]
    out = [
        (jnp.where(even, a, to_first), jnp.where(even, to_second, b))
        for (a, b), (to_first, to_second) in zip(crossed, rolled)
    ]
    return [first + second for first, second in zip(out[::2], out[1::2])]


def triangle_kernel(in_ref, regroup_ref, out_ref, left_ref, right_ref, *, update):
    lane = lax.broadcasted_iota(jnp.int32, (16, 128), 1)
    low = lane < 64
    even = (lane & 32) == 0


    def stacked(side, places):
        tiles = []
        for n in range(4):
            numbers = [device_number(r, 4 * block + n) for r, block in places]
            tiles.append(jnp.concatenate([in_ref[32 * m + 16 * side : 32 * m + 16 * side + 16, :] for m in numbers], axis=0))
        return jnp.concatenate(tiles, axis=1)

    for half in range(2):
        if update == 0:
            places = [(4 * half + r, block) for r in range(4) for block in range(4)]
            regrouped = dot(stacked(1, places), regroup_ref[...], ((1,), (0,))).astype(BF16)
            for m, (r, block) in enumerate(places):
                for g in range(4):
                    row = r * 64 + g * 16
                    tile = regrouped[16 * m : 16 * m + 16, 128 * g : 128 * g + 128]
                    right_ref[row : row + 16, 128 * block : 128 * block + 128] = tile
        else:
            places = [(r, 2 * half + block) for block in range(2) for r in range(8)]
            regrouped = dot(regroup_ref[...], stacked(0, places), ((1,), (1,))).astype(BF16)
            for block in range(2):
                for g in range(4):
                    row = 128 * (2 * half + block)
                    tile = regrouped[128 * g : 128 * g + 128, 128 * block : 128 * block + 128]
                    left_ref[row : row + 128, 128 * g : 128 * g + 128] = tile
    side, full_ref = ((0, left_ref), (1, right_ref))[update]
    places = [(r, block) for r in range(8) for block in range(4)]
    groups = []
    for r, block in places:
        numbers = [device_number(r, 4 * block + n) for n in range(4)]
        groups.append([in_ref[32 * m + 16 * side : 32 * m + 16 * side + 16, :] for m in numbers])
    for (r, block), tiles in zip(places, swap_groups(groups, low, even)):
        for g, tile in enumerate(tiles):
            row = r * 64 + g * 16 if update == 0 else g * 128 + r * 16
            full_ref[row : row + 16, 128 * block : 128 * block + 128] = tile
    products = []
    for half in range(2):
        part = slice(256 * half, 256 * half + 256)
        if update == 0:
            products.append(dot(left_ref[...], right_ref[part, :], ((1,), (1,))).astype(BF16))
        else:
            products.append(dot(left_ref[...], right_ref[:, part], ((1,), (0,))).astype(BF16))
    for half, mixed in enumerate(products):
        places = [(r, block) for r in range(8) for block in range(2)]
        groups = [
            [mixed[r * 64 + 16 * g : r * 64 + 16 * g + 16, 128 * block : 128 * block + 128] for g in range(4)]
            for r, block in places
        ]
        for (r, block), tiles in zip(places, swap_groups(groups, low, even)):
            for n, tile in enumerate(tiles):
                row = device_number(r, 8 * half + 4 * block + n) * 16
                out_ref[row : row + 16, :] = tile


def finish_kernel(mixed_ref, pair_ref, gate_ref, out_weight_ref, gain_ref, *rest, update):
    if update == 0:
        (side_ref, gate_weight_ref, pair_out_ref, out_ref, gate_out_ref, raw_ref, wt_ref, centred_ref,
         normed_ref, half_ref) = rest
    else:
        pair_hbm, raw_ref, pair_out_ref, sems = rest
    if update == 0:
        fill_weights(side_ref, wt_ref, 1)
    for channel in range(0, 128, 16):
        part = mixed_ref[16 * channel : 16 * channel + 256, :].astype(F32).reshape(16, 16, 128)
        for n in range(16):
            raw_ref[24 * (channel + n) : 24 * (channel + n) + 16, :] = part[n]
    out_gain = jnp.broadcast_to(gain_ref[1, update : update + 1, :], (128, 128)).T
    weight = two_blocks(halved(out_weight_ref[update]))
    slabs = [ref.reshape(4, 16, 32, 128) for ref in (pair_ref, gate_ref, pair_out_ref)]
    copies = []
    out_normed = {}
    for s in range(0, 18, 2):
        if s < 16:
            values = jnp.stack([raw_ref[pl.ds(s + n, 128, stride=24), :] for n in range(2)])
            centred = values - jnp.mean(values, axis=1, keepdims=True)
            variance = jnp.mean(centred * centred, axis=1, keepdims=True)
            out_normed[s] = (centred * lax.rsqrt(variance + epsilon) * out_gain).astype(BF16)
        if s == 0:
            continue
        changes = dot(out_normed[s - 2].reshape(256, 128), weight, ((0,), (0,)))
        for n in range(2):
            change = changes[:, 128 * n : 128 * n + 128].reshape(4, 32, 128)
            before, gate = slabs[0][:, s - 2 + n].astype(F32), slabs[1][:, s - 2 + n]
            slabs[2][:, s - 2 + n] = (before + (change + change * gate)).astype(BF16)
        if update == 1 and s % 4 == 0:
            part = pl.ds(s - 4, 4)
            copies.append(pltpu.make_async_copy(slabs[2].at[:, part], pair_hbm.at[:, part], sems.at[s // 4 - 1]))
            copies[-1].start()
    for copy in copies:
        copy.wait()
    if update == 0:
        project(
            pair_out_ref, gain_ref[0, 1:2, :], wt_ref, gate_weight_ref[1],
            (centred_ref, normed_ref, half_ref), out_ref, gate_out_ref, True,
        )


def call(kernel, out, scratch, *operands, hbm=(), hbm_out=False):
    operands = [pltpu.with_memory_space_constraint(a, pltpu.HBM) if n in hbm else a for n, a in enumerate(operands)]
    spaces = [pltpu.HBM if n in hbm else pltpu.VMEM for n in range(len(operands))]
    return pl.pallas_call(
        kernel,
        out_shape=[jax.ShapeDtypeStruct(*one) for one in out],
        in_specs=[pl.BlockSpec(memory_space=space) for space in spaces],
        out_specs=[pl.BlockSpec(memory_space=pltpu.HBM if hbm_out else pltpu.VMEM) for _ in out],
        scratch_shapes=[pltpu.VMEM(*one) if isinstance(one, tuple) else one for one in scratch],
        compiler_params=pltpu.CompilerParams(vmem_limit_bytes=32 * 1024 * 1024),
    )(*operands)


SIDES = ((128, 2, 16, 128), BF16)
MIXED = ((2048, 128), BF16)
PAIR = ((2048, 128), BF16)
GATE = ((2048, 128), F32)
GAIN = ((2, 2, 128), F32)
PROJECT_SCRATCH = [((512, 128), BF16), ((1024, 256), F32), ((2048, 128), BF16), ((5120, 128), F32)]


def exchange(flat):
    pieces = flat.reshape(128, -1, 128)
    moved = lax.all_to_all(pieces, ORDER, split_axis=0, concat_axis=0, tiled=True)
    return moved.reshape(-1, 128)


def on_device(pair_rep, side_weight, gate_weight, out_weight, in_gain, out_gain):
    pair = pair_rep.reshape(PAIR[0])
    side_weight = side_weight.reshape(8, 128, 128)
    sides, gate, gains = call(
        project_kernel,
        [SIDES, GATE, GAIN],
        [PAIR, ((4, 128, 128), BF16), ((128, 128), BF16), *PROJECT_SCRATCH, pltpu.SemaphoreType.DMA((5,))],
        pair, side_weight, gate_weight, in_gain, out_gain,
        hbm=range(5),
    )
    regroup = jnp.asarray(np.eye(512).reshape(4, 4, 32, 512).transpose(1, 0, 2, 3).reshape(512, 512).T, BF16)
    finish_scratch = [((3072, 128), F32)]
    for update in range(2):
        sides = exchange(sides)
        triangle = functools.partial(triangle_kernel, update=update)
        (mixed,) = call(triangle, [MIXED], [((512, 512), BF16)] * 2, sides, regroup)
        mixed = exchange(mixed)
        finish = functools.partial(finish_kernel, update=update)
        operands = (mixed, pair, gate, out_weight, gains)
        if update == 0:
            pair, sides, gate = call(
                finish, [PAIR, SIDES, GATE], finish_scratch + PROJECT_SCRATCH,
                *operands, side_weight, gate_weight,
            )
        else:
            scratch = finish_scratch + [PAIR, pltpu.SemaphoreType.DMA((4,))]
            (pair,) = call(finish, [((4, 16, 32, 128), BF16)], scratch, *operands, hbm_out=True)
    return pair.reshape(pair_rep.shape)


def solution(mesh):
    physical = jax.sharding.Mesh(mesh.devices.reshape((2,) * 7), BITS)
    tile = P(BITS[:3], BITS[3:], None)
    return jax.shard_map(
        on_device, mesh=physical, in_specs=(tile, P(), P(), P(), P(), P()), out_specs=tile, check_vma=False
    )
```

```python
import functools

import jax
import jax.numpy as jnp
import numpy as np
from jax import lax
from jax.experimental import pallas as pl
from jax.experimental.pallas import tpu as pltpu
from jax.sharding import PartitionSpec as P

epsilon = 1e-05
F32 = jnp.float32
BF16 = jnp.bfloat16

BITS = ("y_hi", "y_lo", "z_lo", "x_hi", "x_lo", "z_hi", "core")
ORDER = BITS


def device_number(r, c):
    return 16 * r + c


def dot(a, b, dims):
    return lax.dot_general(a, b, (dims, ((), ())), preferred_element_type=F32)


def ahead(items, produce, consume):
    waiting = None
    for item in items:
        made = produce(item)
        if waiting is not None:
            consume(*waiting)
        waiting = (item, made)
    consume(*waiting)


def two_blocks(matrix):
    zero = jnp.zeros_like(matrix)
    return jnp.concatenate(
        [jnp.concatenate([matrix, zero], axis=1), jnp.concatenate([zero, matrix], axis=1)], axis=0
    )


def side_by_side(ref, n):
    return jnp.concatenate([ref[n : n + 512, :], ref[n + 512 : n + 1024, :]], axis=1)


def norm_rows(pair_ref, gain, centred_ref, normed_ref, prepare):
    row = lax.broadcasted_iota(jnp.int32, (128, 128), 0)
    column = lax.broadcasted_iota(jnp.int32, (128, 128), 1)
    centring = two_blocks(jnp.where(row == column, 127.0 / 128.0, -1.0 / 128.0).astype(BF16))
    average = two_blocks(jnp.full((128, 128), 1.0 / 128.0, BF16))
    for n in range(0, 2048, 1024):
        centred_ref[n // 2 : n // 2 + 512, :] = dot(side_by_side(pair_ref, n), centring, ((1,), (0,)))
    prepare()
    gains = jnp.concatenate([gain, gain], axis=1)

    def spread(n):
        centred = centred_ref[n // 2 : n // 2 + 512, :]
        return dot((centred * centred).astype(BF16), average, ((1,), (0,)))

    def scale(n, variance):
        normed = (centred_ref[n // 2 : n // 2 + 512, :] * lax.rsqrt(variance + epsilon) * gains).astype(BF16)
        normed_ref[n : n + 512, :] = normed[:, :128]
        normed_ref[n + 512 : n + 1024, :] = normed[:, 128:]

    ahead(range(0, 2048, 1024), spread, scale)


def project(pair_ref, gain, wt_ref, gate_weight, refs, out_ref, gate_ref, prepare):
    centred_ref, normed_ref, half_ref = refs
    norm_rows(pair_ref, gain, centred_ref, normed_ref, prepare)
    slabs = normed_ref.reshape(4, 16, 32, 128)
    def product(place):
        s, side = place
        normed = jnp.concatenate([slabs[:, s + n].reshape(128, 128) for n in range(2)], axis=0)
        return dot(wt_ref[256 * side : 256 * side + 256], normed, ((1,), (1,))).reshape(16, 2, 8, 256)

    def gated(place, both):
        s, side = place
        result = (both[:, 0] + both[:, 0] * jnp.tanh(both[:, 1])).reshape(128, 256)
        for n in range(2):
            half_ref[pl.ds(side * 16 + s + n, 128, stride=40), :] = result[:, 128 * n : 128 * n + 128]

    ahead([(s, side) for s in range(0, 16, 2) for side in range(2)], product, gated)
    weight = two_blocks(halved(gate_weight))

    def gate_product(n):
        return dot(side_by_side(normed_ref, n), weight, ((1,), (0,)))

    def gate(n, values):
        values = jnp.tanh(values)
        gate_ref[n : n + 512, :] = values[:, :128]
        gate_ref[n + 512 : n + 1024, :] = values[:, 128:]

    ahead(range(0, 2048, 1024), gate_product, gate)
    for channel in range(0, 128, 16):
        part = half_ref[channel * 40 : channel * 40 + 640, :].reshape(16, 40, 128)[:, :32]
        out_ref[channel : channel + 16] = part.astype(BF16).reshape(16, 2, 16, 128)


def halved(weight):
    return (0.5 * weight.astype(F32)).astype(BF16)


def fill_weights(side_ref, wt_ref, update):
    for side in range(2):
        value, gate = [
            (0.5 * side_ref[4 * update + 2 * side + n].astype(F32)).T.reshape(16, 1, 8, 128) for n in range(2)
        ]
        both = jnp.concatenate([value, gate], axis=1).reshape(256, 128)
        wt_ref[256 * side : 256 * side + 256, :] = both.astype(BF16)


def project_kernel(
    pair_hbm, side_hbm, gate_weight_hbm, gain_hbm, out_gain_hbm, out_ref, gate_ref, gain_ref, pair_ref, side_ref, gate_weight_ref,
    wt_ref, centred_ref, normed_ref, half_ref, sems,
):
    copies = [
        pltpu.make_async_copy(side_hbm.at[pl.ds(0, 4)], side_ref, sems.at[0]),
        pltpu.make_async_copy(pair_hbm, pair_ref, sems.at[1]),
        pltpu.make_async_copy(gate_weight_hbm.at[0], gate_weight_ref, sems.at[2]),
        pltpu.make_async_copy(gain_hbm, gain_ref.at[0], sems.at[3]),
        pltpu.make_async_copy(out_gain_hbm, gain_ref.at[1], sems.at[4]),
    ]
    for copy in copies:
        copy.start()
    copies[0].wait()
    fill_weights(side_ref, wt_ref, 0)
    for copy in copies[1:]:
        copy.wait()
    project(
        pair_ref, gain_ref[0, 0:1, :], wt_ref, gate_weight_ref[...],
        (centred_ref, normed_ref, half_ref), out_ref, gate_ref, lambda: None,
    )


def swap_groups(groups, low, even):
    halves = [pair for t in groups for pair in ((t[0], t[2]), (t[1], t[3]))]
    moved = [pltpu.roll(jnp.where(low, b, a), 64, 1) for a, b in halves]
    halves = [(jnp.where(low, a, m), jnp.where(low, m, b)) for (a, b), m in zip(halves, moved)]
    crossed = []
    for (u0, u2), (u1, u3) in zip(halves[::2], halves[1::2]):
        crossed += [(u0, u1), (u2, u3)]
    rolled = [(pltpu.roll(b, 32, 1), pltpu.roll(a, 96, 1)) for a, b in crossed]
    out = [
        (jnp.where(even, a, to_first), jnp.where(even, to_second, b))
        for (a, b), (to_first, to_second) in zip(crossed, rolled)
    ]
    return [first + second for first, second in zip(out[::2], out[1::2])]


def triangle_kernel(in_ref, regroup_ref, out_ref, left_ref, right_ref, *, update):
    lane = lax.broadcasted_iota(jnp.int32, (16, 128), 1)
    low = lane < 64
    even = (lane & 32) == 0


    def stacked(side, places):
        tiles = []
        for n in range(4):
            numbers = [device_number(r, 4 * block + n) for r, block in places]
            tiles.append(jnp.concatenate([in_ref[32 * m + 16 * side : 32 * m + 16 * side + 16, :] for m in numbers], axis=0))
        return jnp.concatenate(tiles, axis=1)

    for half in range(2):
        if update == 0:
            places = [(4 * half + r, block) for r in range(4) for block in range(4)]
            regrouped = dot(stacked(1, places), regroup_ref[...], ((1,), (0,))).astype(BF16)
            for m, (r, block) in enumerate(places):
                for g in range(4):
                    row = r * 64 + g * 16
                    tile = regrouped[16 * m : 16 * m + 16, 128 * g : 128 * g + 128]
                    right_ref[row : row + 16, 128 * block : 128 * block + 128] = tile
        else:
            places = [(r, 2 * half + block) for block in range(2) for r in range(8)]
            regrouped = dot(regroup_ref[...], stacked(0, places), ((1,), (1,))).astype(BF16)
            for block in range(2):
                for g in range(4):
                    row = 128 * (2 * half + block)
                    tile = regrouped[128 * g : 128 * g + 128, 128 * block : 128 * block + 128]
                    left_ref[row : row + 128, 128 * g : 128 * g + 128] = tile
    side, full_ref = ((0, left_ref), (1, right_ref))[update]
    places = [(r, block) for r in range(8) for block in range(4)]
    groups = []
    for r, block in places:
        numbers = [device_number(r, 4 * block + n) for n in range(4)]
        groups.append([in_ref[32 * m + 16 * side : 32 * m + 16 * side + 16, :] for m in numbers])
    for (r, block), tiles in zip(places, swap_groups(groups, low, even)):
        for g, tile in enumerate(tiles):
            row = r * 64 + g * 16 if update == 0 else g * 128 + r * 16
            full_ref[row : row + 16, 128 * block : 128 * block + 128] = tile
    products = []
    for half in range(2):
        part = slice(256 * half, 256 * half + 256)
        if update == 0:
            products.append(dot(left_ref[...], right_ref[part, :], ((1,), (1,))).astype(BF16))
        else:
            products.append(dot(left_ref[...], right_ref[:, part], ((1,), (0,))).astype(BF16))
    for half, mixed in enumerate(products):
        places = [(r, block) for r in range(8) for block in range(2)]
        groups = [
            [mixed[r * 64 + 16 * g : r * 64 + 16 * g + 16, 128 * block : 128 * block + 128] for g in range(4)]
            for r, block in places
        ]
        for (r, block), tiles in zip(places, swap_groups(groups, low, even)):
            for n, tile in enumerate(tiles):
                row = device_number(r, 8 * half + 4 * block + n) * 16
                out_ref[row : row + 16, :] = tile


def finish_kernel(mixed_ref, pair_ref, gate_ref, out_weight_ref, gain_ref, *rest, update):
    if update == 0:
        (side_ref, gate_weight_ref, pair_out_ref, out_ref, gate_out_ref, raw_ref, wt_ref, centred_ref,
         normed_ref, half_ref) = rest
    else:
        pair_hbm, raw_ref, pair_out_ref, sems = rest
    for channel in range(0, 128, 16):
        part = mixed_ref[16 * channel : 16 * channel + 256, :].astype(F32).reshape(16, 16, 128)
        for n in range(16):
            raw_ref[24 * (channel + n) : 24 * (channel + n) + 16, :] = part[n]
    out_gain = jnp.broadcast_to(gain_ref[1, update : update + 1, :], (128, 128)).T
    weight = two_blocks(halved(out_weight_ref[update]))
    slabs = [ref.reshape(4, 16, 32, 128) for ref in (pair_ref, gate_ref, pair_out_ref)]
    copies = []
    out_normed = {}
    for s in range(0, 18, 2):
        if s < 16:
            values = jnp.stack([raw_ref[pl.ds(s + n, 128, stride=24), :] for n in range(2)])
            centred = values - jnp.mean(values, axis=1, keepdims=True)
            variance = jnp.mean(centred * centred, axis=1, keepdims=True)
            out_normed[s] = (centred * lax.rsqrt(variance + epsilon) * out_gain).astype(BF16)
        if s == 0:
            continue
        changes = dot(out_normed[s - 2].reshape(256, 128), weight, ((0,), (0,)))
        for n in range(2):
            change = changes[:, 128 * n : 128 * n + 128].reshape(4, 32, 128)
            before, gate = slabs[0][:, s - 2 + n].astype(F32), slabs[1][:, s - 2 + n]
            slabs[2][:, s - 2 + n] = (before + (change + change * gate)).astype(BF16)
        if update == 1 and s % 4 == 0:
            part = pl.ds(s - 4, 4)
            copies.append(pltpu.make_async_copy(slabs[2].at[:, part], pair_hbm.at[:, part], sems.at[s // 4 - 1]))
            copies[-1].start()
    for copy in copies:
        copy.wait()
    if update == 0:
        project(
            pair_out_ref, gain_ref[0, 1:2, :], wt_ref, gate_weight_ref[1],
            (centred_ref, normed_ref, half_ref), out_ref, gate_out_ref,
            lambda: fill_weights(side_ref, wt_ref, 1),
        )


def call(kernel, out, scratch, *operands, hbm=(), hbm_out=False):
    operands = [pltpu.with_memory_space_constraint(a, pltpu.HBM) if n in hbm else a for n, a in enumerate(operands)]
    spaces = [pltpu.HBM if n in hbm else pltpu.VMEM for n in range(len(operands))]
    return pl.pallas_call(
        kernel,
        out_shape=[jax.ShapeDtypeStruct(*one) for one in out],
        in_specs=[pl.BlockSpec(memory_space=space) for space in spaces],
        out_specs=[pl.BlockSpec(memory_space=pltpu.HBM if hbm_out else pltpu.VMEM) for _ in out],
        scratch_shapes=[pltpu.VMEM(*one) if isinstance(one, tuple) else one for one in scratch],
        compiler_params=pltpu.CompilerParams(vmem_limit_bytes=32 * 1024 * 1024),
    )(*operands)


SIDES = ((128, 2, 16, 128), BF16)
MIXED = ((2048, 128), BF16)
PAIR = ((2048, 128), BF16)
GATE = ((2048, 128), F32)
GAIN = ((2, 2, 128), F32)
PROJECT_SCRATCH = [((512, 128), BF16), ((1024, 256), F32), ((2048, 128), BF16), ((5120, 128), F32)]


def exchange(flat):
    pieces = flat.reshape(128, -1, 128)
    moved = lax.all_to_all(pieces, ORDER, split_axis=0, concat_axis=0, tiled=True)
    return moved.reshape(-1, 128)


def on_device(pair_rep, side_weight, gate_weight, out_weight, in_gain, out_gain):
    pair = pair_rep.reshape(PAIR[0])
    side_weight = side_weight.reshape(8, 128, 128)
    sides, gate, gains = call(
        project_kernel,
        [SIDES, GATE, GAIN],
        [PAIR, ((4, 128, 128), BF16), ((128, 128), BF16), *PROJECT_SCRATCH, pltpu.SemaphoreType.DMA((5,))],
        pair, side_weight, gate_weight, in_gain, out_gain,
        hbm=range(5),
    )
    regroup = jnp.asarray(np.eye(512).reshape(4, 4, 32, 512).transpose(1, 0, 2, 3).reshape(512, 512).T, BF16)
    finish_scratch = [((3072, 128), F32)]
    for update in range(2):
        sides = exchange(sides)
        triangle = functools.partial(triangle_kernel, update=update)
        (mixed,) = call(triangle, [MIXED], [((512, 512), BF16)] * 2, sides, regroup)
        mixed = exchange(mixed)
        finish = functools.partial(finish_kernel, update=update)
        operands = (mixed, pair, gate, out_weight, gains)
        if update == 0:
            pair, sides, gate = call(
                finish, [PAIR, SIDES, GATE], finish_scratch + PROJECT_SCRATCH,
                *operands, side_weight, gate_weight,
            )
        else:
            scratch = finish_scratch + [PAIR, pltpu.SemaphoreType.DMA((4,))]
            (pair,) = call(finish, [((4, 16, 32, 128), BF16)], scratch, *operands, hbm_out=True)
    return pair.reshape(pair_rep.shape)


def solution(mesh):
    physical = jax.sharding.Mesh(mesh.devices.reshape((2,) * 7), BITS)
    tile = P(BITS[:3], BITS[3:], None)
    return jax.shard_map(
        on_device, mesh=physical, in_specs=(tile, P(), P(), P(), P(), P()), out_specs=tile, check_vma=False
    )
```

```python
import functools

import jax
import jax.numpy as jnp
import numpy as np
from jax import lax
from jax.experimental import pallas as pl
from jax.experimental.pallas import tpu as pltpu
from jax.sharding import PartitionSpec as P

epsilon = 1e-05
F32 = jnp.float32
BF16 = jnp.bfloat16

BITS = ("y_hi", "y_lo", "z_lo", "x_hi", "x_lo", "z_hi", "core")
ORDER = BITS


def device_number(r, c):
    return 16 * r + c


def dot(a, b, dims):
    return lax.dot_general(a, b, (dims, ((), ())), preferred_element_type=F32)


def ahead(items, produce, consume):
    waiting = None
    for item in items:
        made = produce(item)
        if waiting is not None:
            consume(*waiting)
        waiting = (item, made)
    consume(*waiting)


def two_blocks(matrix):
    zero = jnp.zeros_like(matrix)
    return jnp.concatenate(
        [jnp.concatenate([matrix, zero], axis=1), jnp.concatenate([zero, matrix], axis=1)], axis=0
    )


def side_by_side(ref, n):
    return jnp.concatenate([ref[n : n + 512, :], ref[n + 512 : n + 1024, :]], axis=1)


def norm_rows(pair_ref, gain, centred_ref, normed_ref, lanes):
    row = lax.broadcasted_iota(jnp.int32, (128, 128), 0)
    column = lax.broadcasted_iota(jnp.int32, (128, 128), 1)
    centring = two_blocks(jnp.where(row == column, 127.0 / 128.0, -1.0 / 128.0).astype(BF16))
    average = two_blocks(jnp.full((128, 128), 1.0 / 128.0, BF16))
    for n in range(0, 2048, 1024):
        if lanes:
            for m in range(2):
                values = pair_ref[n + 512 * m : n + 512 * m + 512, :].astype(F32)
                centred = values - jnp.mean(values, axis=1, keepdims=True)
                centred_ref[n // 2 : n // 2 + 512, 128 * m : 128 * m + 128] = centred
        else:
            centred_ref[n // 2 : n // 2 + 512, :] = dot(side_by_side(pair_ref, n), centring, ((1,), (0,)))
    gains = jnp.concatenate([gain, gain], axis=1)

    def spread(n):
        centred = centred_ref[n // 2 : n // 2 + 512, :]
        return dot((centred * centred).astype(BF16), average, ((1,), (0,)))

    def scale(n, variance):
        normed = (centred_ref[n // 2 : n // 2 + 512, :] * lax.rsqrt(variance + epsilon) * gains).astype(BF16)
        normed_ref[n : n + 512, :] = normed[:, :128]
        normed_ref[n + 512 : n + 1024, :] = normed[:, 128:]

    ahead(range(0, 2048, 1024), spread, scale)


def project(pair_ref, gain, wt_ref, gate_weight, refs, out_ref, gate_ref, lanes=False):
    centred_ref, normed_ref, half_ref = refs
    norm_rows(pair_ref, gain, centred_ref, normed_ref, lanes)
    slabs = normed_ref.reshape(4, 16, 32, 128)
    def product(place):
        s, side = place
        normed = jnp.concatenate([slabs[:, s + n].reshape(128, 128) for n in range(2)], axis=0)
        return dot(wt_ref[256 * side : 256 * side + 256], normed, ((1,), (1,))).reshape(16, 2, 8, 256)

    def gated(place, both):
        s, side = place
        result = (both[:, 0] + both[:, 0] * jnp.tanh(both[:, 1])).reshape(128, 256)
        for n in range(2):
            half_ref[pl.ds(side * 16 + s + n, 128, stride=40), :] = result[:, 128 * n : 128 * n + 128]

    ahead([(s, side) for s in range(0, 16, 2) for side in range(2)], product, gated)
    weight = two_blocks(halved(gate_weight))

    def gate_product(n):
        return dot(side_by_side(normed_ref, n), weight, ((1,), (0,)))

    def gate(n, values):
        values = jnp.tanh(values).astype(BF16)
        gate_ref[n : n + 512, :] = values[:, :128]
        gate_ref[n + 512 : n + 1024, :] = values[:, 128:]

    ahead(range(0, 2048, 1024), gate_product, gate)
    for channel in range(0, 128, 16):
        part = half_ref[channel * 40 : channel * 40 + 640, :].reshape(16, 40, 128)[:, :32]
        out_ref[channel : channel + 16] = part.astype(BF16).reshape(16, 2, 16, 128)


def halved(weight):
    return (0.5 * weight.astype(F32)).astype(BF16)


def fill_weights(side_ref, wt_ref, update):
    for side in range(2):
        value, gate = [
            (0.5 * side_ref[4 * update + 2 * side + n].astype(F32)).T.reshape(16, 1, 8, 128) for n in range(2)
        ]
        both = jnp.concatenate([value, gate], axis=1).reshape(256, 128)
        wt_ref[256 * side : 256 * side + 256, :] = both.astype(BF16)


def project_kernel(
    pair_hbm, side_hbm, gate_weight_hbm, gain_hbm, out_gain_hbm, out_ref, gate_ref, gain_ref, pair_ref, side_ref, gate_weight_ref,
    wt_ref, centred_ref, normed_ref, half_ref, sems,
):
    copies = [
        pltpu.make_async_copy(pair_hbm, pair_ref, sems.at[1]),
        pltpu.make_async_copy(side_hbm.at[pl.ds(0, 4)], side_ref, sems.at[0]),
        pltpu.make_async_copy(gate_weight_hbm.at[0], gate_weight_ref, sems.at[2]),
        pltpu.make_async_copy(gain_hbm, gain_ref.at[0], sems.at[3]),
        pltpu.make_async_copy(out_gain_hbm, gain_ref.at[1], sems.at[4]),
    ]
    for copy in copies:
        copy.start()
    copies[1].wait()
    fill_weights(side_ref, wt_ref, 0)
    for copy in copies[:1] + copies[2:]:
        copy.wait()
    project(
        pair_ref, gain_ref[0, 0:1, :], wt_ref, gate_weight_ref[...],
        (centred_ref, normed_ref, half_ref), out_ref, gate_ref, True,
    )


def swap_groups(groups, low, even):
    halves = [pair for t in groups for pair in ((t[0], t[2]), (t[1], t[3]))]
    moved = [pltpu.roll(jnp.where(low, b, a), 64, 1) for a, b in halves]
    halves = [(jnp.where(low, a, m), jnp.where(low, m, b)) for (a, b), m in zip(halves, moved)]
    crossed = []
    for (u0, u2), (u1, u3) in zip(halves[::2], halves[1::2]):
        crossed += [(u0, u1), (u2, u3)]
    rolled = [(pltpu.roll(b, 32, 1), pltpu.roll(a, 96, 1)) for a, b in crossed]
    out = [
        (jnp.where(even, a, to_first), jnp.where(even, to_second, b))
        for (a, b), (to_first, to_second) in zip(crossed, rolled)
    ]
    return [first + second for first, second in zip(out[::2], out[1::2])]


def triangle_kernel(in_ref, regroup_ref, out_ref, left_ref, right_ref, *, update):
    lane = lax.broadcasted_iota(jnp.int32, (16, 128), 1)
    low = lane < 64
    even = (lane & 32) == 0


    def stacked(side, places):
        tiles = []
        for n in range(4):
            numbers = [device_number(r, 4 * block + n) for r, block in places]
            tiles.append(jnp.concatenate([in_ref[32 * m + 16 * side : 32 * m + 16 * side + 16, :] for m in numbers], axis=0))
        return jnp.concatenate(tiles, axis=1)

    for half in range(2):
        if update == 0:
            places = [(4 * half + r, block) for r in range(4) for block in range(4)]
            regrouped = dot(stacked(1, places), regroup_ref[...], ((1,), (0,))).astype(BF16)
            for m, (r, block) in enumerate(places):
                for g in range(4):
                    row = r * 64 + g * 16
                    tile = regrouped[16 * m : 16 * m + 16, 128 * g : 128 * g + 128]
                    right_ref[row : row + 16, 128 * block : 128 * block + 128] = tile
        else:
            places = [(r, 2 * half + block) for block in range(2) for r in range(8)]
            regrouped = dot(regroup_ref[...], stacked(0, places), ((1,), (1,))).astype(BF16)
            for block in range(2):
                for g in range(4):
                    row = 128 * (2 * half + block)
                    tile = regrouped[128 * g : 128 * g + 128, 128 * block : 128 * block + 128]
                    left_ref[row : row + 128, 128 * g : 128 * g + 128] = tile
    side, full_ref = ((0, left_ref), (1, right_ref))[update]
    places = [(r, block) for r in range(8) for block in range(4)]
    groups = []
    for r, block in places:
        numbers = [device_number(r, 4 * block + n) for n in range(4)]
        groups.append([in_ref[32 * m + 16 * side : 32 * m + 16 * side + 16, :] for m in numbers])
    for (r, block), tiles in zip(places, swap_groups(groups, low, even)):
        for g, tile in enumerate(tiles):
            row = r * 64 + g * 16 if update == 0 else g * 128 + r * 16
            full_ref[row : row + 16, 128 * block : 128 * block + 128] = tile
    products = []
    for half in range(2):
        part = slice(256 * half, 256 * half + 256)
        if update == 0:
            products.append(dot(left_ref[...], right_ref[part, :], ((1,), (1,))).astype(BF16))
        else:
            products.append(dot(left_ref[...], right_ref[:, part], ((1,), (0,))).astype(BF16))
    for half, mixed in enumerate(products):
        places = [(r, block) for r in range(8) for block in range(2)]
        groups = [
            [mixed[r * 64 + 16 * g : r * 64 + 16 * g + 16, 128 * block : 128 * block + 128] for g in range(4)]
            for r, block in places
        ]
        for (r, block), tiles in zip(places, swap_groups(groups, low, even)):
            for n, tile in enumerate(tiles):
                row = device_number(r, 8 * half + 4 * block + n) * 16
                out_ref[row : row + 16, :] = tile


def finish_kernel(mixed_ref, pair_ref, gate_ref, out_weight_ref, gain_ref, *rest, update):
    if update == 0:
        (side_ref, gate_weight_ref, pair_out_ref, out_ref, gate_out_ref, raw_ref, wt_ref, centred_ref,
         normed_ref, half_ref) = rest
    else:
        pair_hbm, raw_ref, pair_out_ref, sems = rest
    if update == 0:
        fill_weights(side_ref, wt_ref, 1)
    for channel in range(0, 128, 16):
        part = mixed_ref[16 * channel : 16 * channel + 256, :].astype(F32).reshape(16, 16, 128)
        for n in range(16):
            raw_ref[24 * (channel + n) : 24 * (channel + n) + 16, :] = part[n]
    out_gain = jnp.broadcast_to(gain_ref[1, update : update + 1, :], (128, 128)).T
    weight = two_blocks(halved(out_weight_ref[update]))
    slabs = [ref.reshape(4, 16, 32, 128) for ref in (pair_ref, gate_ref, pair_out_ref)]
    copies = []
    out_normed = {}
    for s in range(0, 18, 2):
        if s < 16:
            values = jnp.stack([raw_ref[pl.ds(s + n, 128, stride=24), :] for n in range(2)])
            centred = values - jnp.mean(values, axis=1, keepdims=True)
            variance = jnp.mean(centred * centred, axis=1, keepdims=True)
            out_normed[s] = (centred * lax.rsqrt(variance + epsilon) * out_gain).astype(BF16)
        if s == 0:
            continue
        changes = dot(out_normed[s - 2].reshape(256, 128), weight, ((0,), (0,)))
        for n in range(2):
            change = changes[:, 128 * n : 128 * n + 128].reshape(4, 32, 128)
            before, gate = slabs[0][:, s - 2 + n].astype(F32), slabs[1][:, s - 2 + n].astype(F32)
            slabs[2][:, s - 2 + n] = (before + (change + change * gate)).astype(BF16)
        if update == 1 and s % 4 == 0:
            part = pl.ds(s - 4, 4)
            copies.append(pltpu.make_async_copy(slabs[2].at[:, part], pair_hbm.at[:, part], sems.at[s // 4 - 1]))
            copies[-1].start()
    for copy in copies:
        copy.wait()
    if update == 0:
        project(
            pair_out_ref, gain_ref[0, 1:2, :], wt_ref, gate_weight_ref[1],
            (centred_ref, normed_ref, half_ref), out_ref, gate_out_ref,
        )


def call(kernel, out, scratch, *operands, hbm=(), hbm_out=False):
    operands = [pltpu.with_memory_space_constraint(a, pltpu.HBM) if n in hbm else a for n, a in enumerate(operands)]
    spaces = [pltpu.HBM if n in hbm else pltpu.VMEM for n in range(len(operands))]
    return pl.pallas_call(
        kernel,
        out_shape=[jax.ShapeDtypeStruct(*one) for one in out],
        in_specs=[pl.BlockSpec(memory_space=space) for space in spaces],
        out_specs=[pl.BlockSpec(memory_space=pltpu.HBM if hbm_out else pltpu.VMEM) for _ in out],
        scratch_shapes=[pltpu.VMEM(*one) if isinstance(one, tuple) else one for one in scratch],
        compiler_params=pltpu.CompilerParams(vmem_limit_bytes=32 * 1024 * 1024),
    )(*operands)


SIDES = ((128, 2, 16, 128), BF16)
MIXED = ((2048, 128), BF16)
PAIR = ((2048, 128), BF16)
GATE = ((2048, 128), BF16)
GAIN = ((2, 2, 128), F32)
PROJECT_SCRATCH = [((512, 128), BF16), ((1024, 256), F32), ((2048, 128), BF16), ((5120, 128), F32)]


def exchange(flat):
    pieces = flat.reshape(128, -1, 128)
    moved = lax.all_to_all(pieces, ORDER, split_axis=0, concat_axis=0, tiled=True)
    return moved.reshape(-1, 128)


def on_device(pair_rep, side_weight, gate_weight, out_weight, in_gain, out_gain):
    pair = pair_rep.reshape(PAIR[0])
    side_weight = side_weight.reshape(8, 128, 128)
    sides, gate, gains = call(
        project_kernel,
        [SIDES, GATE, GAIN],
        [PAIR, ((4, 128, 128), BF16), ((128, 128), BF16), *PROJECT_SCRATCH, pltpu.SemaphoreType.DMA((5,))],
        pair, side_weight, gate_weight, in_gain, out_gain,
        hbm=range(5),
    )
    regroup = jnp.asarray(np.eye(512).reshape(4, 4, 32, 512).transpose(1, 0, 2, 3).reshape(512, 512).T, BF16)
    finish_scratch = [((3072, 128), F32)]
    for update in range(2):
        sides = exchange(sides)
        triangle = functools.partial(triangle_kernel, update=update)
        (mixed,) = call(triangle, [MIXED], [((512, 512), BF16)] * 2, sides, regroup)
        mixed = exchange(mixed)
        finish = functools.partial(finish_kernel, update=update)
        operands = (mixed, pair, gate, out_weight, gains)
        if update == 0:
            pair, sides, gate = call(
                finish, [PAIR, SIDES, GATE], finish_scratch + PROJECT_SCRATCH,
                *operands, side_weight, gate_weight,
            )
        else:
            scratch = finish_scratch + [PAIR, pltpu.SemaphoreType.DMA((4,))]
            (pair,) = call(finish, [((4, 16, 32, 128), BF16)], scratch, *operands, hbm_out=True)
    return pair.reshape(pair_rep.shape)


def solution(mesh):
    physical = jax.sharding.Mesh(mesh.devices.reshape((2,) * 7), BITS)
    tile = P(BITS[:3], BITS[3:], None)
    return jax.shard_map(
        on_device, mesh=physical, in_specs=(tile, P(), P(), P(), P(), P()), out_specs=tile, check_vma=False
    )
```

```python
import functools

import jax
import jax.numpy as jnp
import numpy as np
from jax import lax
from jax.experimental import pallas as pl
from jax.experimental.pallas import tpu as pltpu
from jax.sharding import PartitionSpec as P

epsilon = 1e-05
F32 = jnp.float32
BF16 = jnp.bfloat16

BITS = ("y_hi", "y_lo", "z_lo", "x_hi", "x_lo", "z_hi", "core")
ORDER = BITS


def device_number(r, c):
    return 16 * r + c


def dot(a, b, dims):
    return lax.dot_general(a, b, (dims, ((), ())), preferred_element_type=F32)


def ahead(items, produce, consume):
    waiting = None
    for item in items:
        made = produce(item)
        if waiting is not None:
            consume(*waiting)
        waiting = (item, made)
    consume(*waiting)


def two_blocks(matrix):
    zero = jnp.zeros_like(matrix)
    return jnp.concatenate(
        [jnp.concatenate([matrix, zero], axis=1), jnp.concatenate([zero, matrix], axis=1)], axis=0
    )


def side_by_side(ref, n):
    return jnp.concatenate([ref[n : n + 512, :], ref[n + 512 : n + 1024, :]], axis=1)


def norm_rows(pair_ref, gain, centred_ref, normed_ref, lanes):
    row = lax.broadcasted_iota(jnp.int32, (128, 128), 0)
    column = lax.broadcasted_iota(jnp.int32, (128, 128), 1)
    centring = two_blocks(jnp.where(row == column, 127.0 / 128.0, -1.0 / 128.0).astype(BF16))
    average = two_blocks(jnp.full((128, 128), 1.0 / 128.0, BF16))
    for n in range(0, 2048, 1024):
        if lanes:
            for m in range(2):
                values = pair_ref[n + 512 * m : n + 512 * m + 512, :].astype(F32)
                centred = values - jnp.mean(values, axis=1, keepdims=True)
                centred_ref[n // 2 : n // 2 + 512, 128 * m : 128 * m + 128] = centred
        else:
            centred_ref[n // 2 : n // 2 + 512, :] = dot(side_by_side(pair_ref, n), centring, ((1,), (0,)))
    gains = jnp.concatenate([gain, gain], axis=1)

    def spread(n):
        centred = centred_ref[n // 2 : n // 2 + 512, :]
        return dot((centred * centred).astype(BF16), average, ((1,), (0,)))

    def scale(n, variance):
        normed = (centred_ref[n // 2 : n // 2 + 512, :] * lax.rsqrt(variance + epsilon) * gains).astype(BF16)
        normed_ref[n : n + 512, :] = normed[:, :128]
        normed_ref[n + 512 : n + 1024, :] = normed[:, 128:]

    ahead(range(0, 2048, 1024), spread, scale)


def project(pair_ref, gain, wt_ref, gate_weight, refs, out_ref, gate_ref, lanes=False):
    centred_ref, normed_ref, half_ref = refs
    norm_rows(pair_ref, gain, centred_ref, normed_ref, lanes)
    slabs = normed_ref.reshape(4, 16, 32, 128)
    def product(place):
        s, side = place
        normed = jnp.concatenate([slabs[:, s + n].reshape(128, 128) for n in range(2)], axis=0)
        return dot(wt_ref[256 * side : 256 * side + 256], normed, ((1,), (1,))).reshape(16, 2, 8, 256)

    def gated(place, both):
        s, side = place
        result = (both[:, 0] + both[:, 0] * jnp.tanh(both[:, 1])).reshape(128, 256)
        for n in range(2):
            half_ref[pl.ds(side * 16 + s + n, 128, stride=40), :] = result[:, 128 * n : 128 * n + 128]

    ahead([(s, side) for s in range(0, 16, 2) for side in range(2)], product, gated)
    weight = two_blocks(halved(gate_weight))

    def gate_product(n):
        return dot(side_by_side(normed_ref, n), weight, ((1,), (0,)))

    def gate(n, values):
        values = jnp.tanh(values)
        gate_ref[n : n + 512, :] = values[:, :128]
        gate_ref[n + 512 : n + 1024, :] = values[:, 128:]

    ahead(range(0, 2048, 1024), gate_product, gate)
    for channel in range(0, 128, 16):
        part = half_ref[channel * 40 : channel * 40 + 640, :].reshape(16, 40, 128)[:, :32]
        out_ref[channel : channel + 16] = part.astype(BF16).reshape(16, 2, 16, 128)


def halved(weight):
    return (0.5 * weight.astype(F32)).astype(BF16)


def fill_weights(side_ref, wt_ref, update):
    for side in range(2):
        value, gate = [
            (0.5 * side_ref[4 * update + 2 * side + n].astype(F32)).T.reshape(16, 1, 8, 128) for n in range(2)
        ]
        both = jnp.concatenate([value, gate], axis=1).reshape(256, 128)
        wt_ref[256 * side : 256 * side + 256, :] = both.astype(BF16)


def project_kernel(
    pair_hbm, side_hbm, gate_weight_hbm, gain_hbm, out_gain_hbm, out_ref, gate_ref, gain_ref, pair_ref, side_ref, gate_weight_ref,
    wt_ref, centred_ref, normed_ref, half_ref, sems,
):
    copies = [
        pltpu.make_async_copy(side_hbm.at[pl.ds(0, 4)], side_ref, sems.at[0]),
        pltpu.make_async_copy(pair_hbm, pair_ref, sems.at[1]),
        pltpu.make_async_copy(gate_weight_hbm.at[0], gate_weight_ref, sems.at[2]),
        pltpu.make_async_copy(gain_hbm, gain_ref.at[0], sems.at[3]),
        pltpu.make_async_copy(out_gain_hbm, gain_ref.at[1], sems.at[4]),
    ]
    for copy in copies:
        copy.start()
    copies[0].wait()
    fill_weights(side_ref, wt_ref, 0)
    for copy in copies[1:]:
        copy.wait()
    project(
        pair_ref, gain_ref[0, 0:1, :], wt_ref, gate_weight_ref[...],
        (centred_ref, normed_ref, half_ref), out_ref, gate_ref, True,
    )


def swap_groups(groups, low, even):
    halves = [pair for t in groups for pair in ((t[0], t[2]), (t[1], t[3]))]
    moved = [pltpu.roll(jnp.where(low, b, a), 64, 1) for a, b in halves]
    halves = [(jnp.where(low, a, m), jnp.where(low, m, b)) for (a, b), m in zip(halves, moved)]
    crossed = []
    for (u0, u2), (u1, u3) in zip(halves[::2], halves[1::2]):
        crossed += [(u0, u1), (u2, u3)]
    rolled = [(pltpu.roll(b, 32, 1), pltpu.roll(a, 96, 1)) for a, b in crossed]
    out = [
        (jnp.where(even, a, to_first), jnp.where(even, to_second, b))
        for (a, b), (to_first, to_second) in zip(crossed, rolled)
    ]
    return [first + second for first, second in zip(out[::2], out[1::2])]


def triangle_kernel(in_ref, regroup_ref, out_ref, left_ref, right_ref, *, update):
    lane = lax.broadcasted_iota(jnp.int32, (16, 128), 1)
    low = lane < 64
    even = (lane & 32) == 0


    def stacked(side, places):
        tiles = []
        for n in range(4):
            numbers = [device_number(r, 4 * block + n) for r, block in places]
            tiles.append(jnp.concatenate([in_ref[32 * m + 16 * side : 32 * m + 16 * side + 16, :] for m in numbers], axis=0))
        return jnp.concatenate(tiles, axis=1)

    side, full_ref = ((0, left_ref), (1, right_ref))[update]
    for half in range(2):
        if update == 0:
            places = [(4 * half + r, block) for r in range(4) for block in range(4)]
            regrouped = dot(stacked(1, places), regroup_ref[...], ((1,), (0,))).astype(BF16)
            for m, (r, block) in enumerate(places):
                for g in range(4):
                    row = r * 64 + g * 16
                    tile = regrouped[16 * m : 16 * m + 16, 128 * g : 128 * g + 128]
                    right_ref[row : row + 16, 128 * block : 128 * block + 128] = tile
        else:
            places = [(r, 2 * half + block) for block in range(2) for r in range(8)]
            regrouped = dot(regroup_ref[...], stacked(0, places), ((1,), (1,))).astype(BF16)
            for block in range(2):
                for g in range(4):
                    row = 128 * (2 * half + block)
                    tile = regrouped[128 * g : 128 * g + 128, 128 * block : 128 * block + 128]
                    left_ref[row : row + 128, 128 * g : 128 * g + 128] = tile
        places = [(r, block) for r in range(4 * half, 4 * half + 4) for block in range(4)]
        groups = []
        for r, block in places:
            numbers = [device_number(r, 4 * block + n) for n in range(4)]
            groups.append([in_ref[32 * m + 16 * side : 32 * m + 16 * side + 16, :] for m in numbers])
        for (r, block), tiles in zip(places, swap_groups(groups, low, even)):
            for g, tile in enumerate(tiles):
                row = r * 64 + g * 16 if update == 0 else g * 128 + r * 16
                full_ref[row : row + 16, 128 * block : 128 * block + 128] = tile
    products = []
    for half in range(2):
        part = slice(256 * half, 256 * half + 256)
        if update == 0:
            products.append(dot(left_ref[...], right_ref[part, :], ((1,), (1,))).astype(BF16))
        else:
            products.append(dot(left_ref[...], right_ref[:, part], ((1,), (0,))).astype(BF16))
    for half, mixed in enumerate(products):
        places = [(r, block) for r in range(8) for block in range(2)]
        groups = [
            [mixed[r * 64 + 16 * g : r * 64 + 16 * g + 16, 128 * block : 128 * block + 128] for g in range(4)]
            for r, block in places
        ]
        for (r, block), tiles in zip(places, swap_groups(groups, low, even)):
            for n, tile in enumerate(tiles):
                row = device_number(r, 8 * half + 4 * block + n) * 16
                out_ref[row : row + 16, :] = tile


def finish_kernel(mixed_ref, pair_ref, gate_ref, out_weight_ref, gain_ref, *rest, update):
    if update == 0:
        (side_ref, gate_weight_ref, pair_out_ref, out_ref, gate_out_ref, raw_ref, wt_ref, centred_ref,
         normed_ref, half_ref) = rest
    else:
        pair_hbm, raw_ref, pair_out_ref, sems = rest
    if update == 0:
        fill_weights(side_ref, wt_ref, 1)
    for channel in range(0, 128, 16):
        part = mixed_ref[16 * channel : 16 * channel + 256, :].astype(F32).reshape(16, 16, 128)
        for n in range(16):
            raw_ref[24 * (channel + n) : 24 * (channel + n) + 16, :] = part[n]
    out_gain = jnp.broadcast_to(gain_ref[1, update : update + 1, :], (128, 128)).T
    weight = two_blocks(halved(out_weight_ref[update]))
    slabs = [ref.reshape(4, 16, 32, 128) for ref in (pair_ref, gate_ref, pair_out_ref)]
    copies = []
    out_normed = {}
    for s in range(0, 18, 2):
        if s < 16:
            values = jnp.stack([raw_ref[pl.ds(s + n, 128, stride=24), :] for n in range(2)])
            centred = values - jnp.mean(values, axis=1, keepdims=True)
            variance = jnp.mean(centred * centred, axis=1, keepdims=True)
            out_normed[s] = (centred * lax.rsqrt(variance + epsilon) * out_gain).astype(BF16)
        if s == 0:
            continue
        changes = dot(out_normed[s - 2].reshape(256, 128), weight, ((0,), (0,)))
        for n in range(2):
            change = changes[:, 128 * n : 128 * n + 128].reshape(4, 32, 128)
            before, gate = slabs[0][:, s - 2 + n].astype(F32), slabs[1][:, s - 2 + n]
            slabs[2][:, s - 2 + n] = (before + (change + change * gate)).astype(BF16)
        if update == 1 and s % 4 == 0:
            part = pl.ds(s - 4, 4)
            copies.append(pltpu.make_async_copy(slabs[2].at[:, part], pair_hbm.at[:, part], sems.at[s // 4 - 1]))
            copies[-1].start()
    for copy in copies:
        copy.wait()
    if update == 0:
        project(
            pair_out_ref, gain_ref[0, 1:2, :], wt_ref, gate_weight_ref[1],
            (centred_ref, normed_ref, half_ref), out_ref, gate_out_ref,
        )


def call(kernel, out, scratch, *operands, hbm=(), hbm_out=False):
    operands = [pltpu.with_memory_space_constraint(a, pltpu.HBM) if n in hbm else a for n, a in enumerate(operands)]
    spaces = [pltpu.HBM if n in hbm else pltpu.VMEM for n in range(len(operands))]
    return pl.pallas_call(
        kernel,
        out_shape=[jax.ShapeDtypeStruct(*one) for one in out],
        in_specs=[pl.BlockSpec(memory_space=space) for space in spaces],
        out_specs=[pl.BlockSpec(memory_space=pltpu.HBM if hbm_out else pltpu.VMEM) for _ in out],
        scratch_shapes=[pltpu.VMEM(*one) if isinstance(one, tuple) else one for one in scratch],
        compiler_params=pltpu.CompilerParams(vmem_limit_bytes=32 * 1024 * 1024),
    )(*operands)


SIDES = ((128, 2, 16, 128), BF16)
MIXED = ((2048, 128), BF16)
PAIR = ((2048, 128), BF16)
GATE = ((2048, 128), F32)
GAIN = ((2, 2, 128), F32)
PROJECT_SCRATCH = [((512, 128), BF16), ((1024, 256), F32), ((2048, 128), BF16), ((5120, 128), F32)]


def exchange(flat):
    pieces = flat.reshape(128, -1, 128)
    moved = lax.all_to_all(pieces, ORDER, split_axis=0, concat_axis=0, tiled=True)
    return moved.reshape(-1, 128)


def on_device(pair_rep, side_weight, gate_weight, out_weight, in_gain, out_gain):
    pair = pair_rep.reshape(PAIR[0])
    side_weight = side_weight.reshape(8, 128, 128)
    sides, gate, gains = call(
        project_kernel,
        [SIDES, GATE, GAIN],
        [PAIR, ((4, 128, 128), BF16), ((128, 128), BF16), *PROJECT_SCRATCH, pltpu.SemaphoreType.DMA((5,))],
        pair, side_weight, gate_weight, in_gain, out_gain,
        hbm=range(5),
    )
    regroup = jnp.asarray(np.eye(512).reshape(4, 4, 32, 512).transpose(1, 0, 2, 3).reshape(512, 512).T, BF16)
    finish_scratch = [((3072, 128), F32)]
    for update in range(2):
        sides = exchange(sides)
        triangle = functools.partial(triangle_kernel, update=update)
        (mixed,) = call(triangle, [MIXED], [((512, 512), BF16)] * 2, sides, regroup)
        mixed = exchange(mixed)
        finish = functools.partial(finish_kernel, update=update)
        operands = (mixed, pair, gate, out_weight, gains)
        if update == 0:
            pair, sides, gate = call(
                finish, [PAIR, SIDES, GATE], finish_scratch + PROJECT_SCRATCH,
                *operands, side_weight, gate_weight,
            )
        else:
            scratch = finish_scratch + [PAIR, pltpu.SemaphoreType.DMA((4,))]
            (pair,) = call(finish, [((4, 16, 32, 128), BF16)], scratch, *operands, hbm_out=True)
    return pair.reshape(pair_rep.shape)


def solution(mesh):
    physical = jax.sharding.Mesh(mesh.devices.reshape((2,) * 7), BITS)
    tile = P(BITS[:3], BITS[3:], None)
    return jax.shard_map(
        on_device, mesh=physical, in_specs=(tile, P(), P(), P(), P(), P()), out_specs=tile, check_vma=False
    )
```
